128 devices in a mesh: pipe: 2 (over x_lo), tensor: 4 (over x_hi, core), dp: 16 (over z, y).
Axes of the slice: x: 4 (x_hi: 2, x_lo: 2; x = x_hi * 2 + x_lo), y: 4, z: 4, core: 2. Of those that a mesh axis runs over, the one named last changes fastest.
Arguments:
- layer_inputs: bfloat16 [2, 2048, 8192], P('pipe', 'dp', 'tensor'), may hold values from -6 to 6
- norm_gain: float32 [2, 8192], P('pipe', 'tensor'), may hold values from 0.25 to 1.75
- value_weight: bfloat16 [2, 8192, 512], P('pipe', ('tensor', 'dp')), may hold values from -0.0625 to 0.0625
- out_weight: bfloat16 [2, 4096, 8192], P('pipe', None, ('tensor', 'dp')), may hold values from -0.09375 to 0.09375
- scores: bfloat16 [2, 16, 4, 32, 32, 32], P('pipe', 'dp', None, 'tensor'), may hold values from -12 to 312, as said below
- head_weight: bfloat16 [8192], P('tensor'), may hold values from -0.0625 to 0.0625
- lengths: int32 [16, 4], replicated, may hold values from 1 to 32, 112 in all within a row
- returns: float32 [2048], P('dp'), may hold values from 0.5 to 54, as said below
- response_mask: int32 [2048], P('dp'), may hold values 0 or 1
Outputs:
- grad_out: bfloat16 [2, 4096, 8192], P('pipe', None, ('tensor', 'dp'))
- grad_value: bfloat16 [2, 8192, 512], P('pipe', ('tensor', 'dp'))
- grad_gain: float32 [2, 8192], P('pipe', ('tensor', 'dp'))
The draws below stay inside these ranges and needn't reach their ends.
Inputs may be any that keep to these rules, and one draw needn't show every extreme that they name: `scores`: every query and key pair holds a logit, also above the diagonal and past a microbatch's length; those entries are only removed by the mask of the attention step. Positive returns.
All inputs are finite; a program needn't handle non-finite values. No bound on the sum of `response_mask` on one device may be relied on, other than what follows from the above.
Results may differ from the reference program's by a relative error of at most 0.015.
Values may be sent and summed in bfloat16 or wider, within the bound.
A program may use at most 192 MiB of HBM per device.

```python
import math
import jax
import jax.numpy as jnp
import numpy as np
from jax import lax

D = 8192
HD = 128
HEADS = 32
KVH = 4
MB = 4
LMAX = 32
SECTIONS = 2
REPLICAS = 16
TOKENS = 2048


def draw_scores(key, part):
    key = jax.random.fold_in(key, 7)
    first_key = jax.random.fold_in(key, 0)
    shape = (SECTIONS, REPLICAS, MB, HEADS, LMAX, LMAX)
    logits = 1.5 * jnp.clip(jax.random.normal(first_key, shape, jnp.float32), -7.0, 7.0)
    return logits.astype(jnp.bfloat16)


def draw_returns(key, part):
    key = jax.random.fold_in(key, 11)
    replica_of = (jnp.arange(TOKENS, dtype=jnp.int32) // (MB * LMAX)).astype(jnp.float32)
    ramp = 1.0 + 2.0 * replica_of / max(REPLICAS - 1, 1)
    base = jax.random.uniform(key, (TOKENS,), jnp.float32, 0.5, 6.0)
    values = ramp * base
    return values.astype(jnp.float32)


def touch_ends(values, rng, low, largest):
    longest = values.shape.index(max(values.shape))
    spots = []
    for shift in (0, 1):
        where = [jax.random.randint(jax.random.fold_in(rng, axis), (), 0, length) for axis, length in enumerate(values.shape)]
        where[longest] = (where[longest] + shift) % values.shape[longest]
        spots.append(tuple(where))
    return values.at[spots[0]].set(low).at[spots[1]].set(largest)


def levels(rng, shape, cuts, low, high):
    def one(axis_at, blocks):
        heights = jax.random.uniform(jax.random.fold_in(jax.random.fold_in(rng, 6), axis_at), (blocks,), jnp.float32, low / len(cuts), high / len(cuts))
        return jnp.repeat(jnp.exp(heights), shape[axis_at] // blocks).reshape((-1,) + (1,) * (len(shape) - axis_at - 1))

    level = one(*cuts[0])
    for cut in cuts[1:]:
        level = level * one(*cut)
    return level


def length_profile(count, total, most, lean):
    weights = [(1 << 20) // math.isqrt(standing ** lean) + 1 for standing in range(2, count + 1)]
    spare, given = total - most - (count - 1), [1] * (count - 1)
    while spare > 0:
        free = [i for i in range(count - 1) if given[i] < most]
        whole, budget = sum([weights[i] for i in free]), spare
        for i in free:
            addition = min(most - given[i], max(1, budget * weights[i] // whole), spare)
            given[i] = given[i] + addition
            spare = spare - addition
    return np.array([most] + given)


def uneven_parts(key, count, total, reach, skew):
    if count == 2:
        one = jax.random.randint(key, (), max(1, total - reach), min(reach, total - 1) + 1)
        return jnp.stack([one, total - one])
    tallies = jnp.asarray(length_profile(count, total, reach, skew), jnp.int32)
    twos = (count - 1) // 2
    source_of, sink = tallies[1:1 + 2 * twos:2], tallies[2:2 + 2 * twos:2]
    slack = jnp.minimum(source_of - 1, reach - sink)
    shifted = jax.random.randint(jax.random.fold_in(key, 1), (twos,), 0, 1 << 20) % (slack + 1)
    tallies = tallies.at[1:1 + 2 * twos:2].set(source_of - shifted).at[2:2 + 2 * twos:2].set(sink + shifted)
    return tallies[jax.random.permutation(jax.random.fold_in(key, 2), count)]


def scatter_about(rng, extent, width, bound, pieces=(), held_as=jnp.bfloat16):
    drawn = jax.random.normal(rng, extent, jnp.float32) * width
    if len(pieces) > 0:
        drawn = levels(rng, extent, pieces, -0.22, 0.18) * drawn
    return jnp.clip(drawn, min=-bound, max=bound).astype(held_as)


def setup_inputs(seed: int = 0) -> dict:
    arg_keys = jax.random.split(jax.random.key(seed), 10)
    layer_inputs = scatter_about(arg_keys[0], (SECTIONS, TOKENS, D), 1.0, 6.0, ((0, 2), (1, 16), (2, 4)))
    norm_gain = jnp.clip(1.0 + 0.15 * jax.random.normal(arg_keys[1], (SECTIONS, D), jnp.float32), 0.25, 1.75)
    value_weight = scatter_about(arg_keys[2], (SECTIONS, D, KVH * HD), D ** -0.5, 0.0625, ((0, 2), (1, 64)))
    out_weight = scatter_about(arg_keys[3], (SECTIONS, HEADS * HD, D), (HEADS * HD) ** -0.5, 0.09375, ((0, 2), (2, 64)))
    scores = draw_scores(jax.random.fold_in(arg_keys[9], 71), 0)
    head_weight = scatter_about(arg_keys[5], (D,), D ** -0.5, 0.0625, ((0, 4),))
    lengths = jax.vmap(lambda own: uneven_parts(own, MB, MB * LMAX * 7 // 8, LMAX, 0))(jax.random.split(arg_keys[6], REPLICAS)).reshape((REPLICAS, MB)).astype(jnp.int32)
    returns = draw_returns(jax.random.fold_in(arg_keys[9], 71), 0)
    response_mask = touch_ends((jax.random.randint(arg_keys[8], (TOKENS,), 0, 4) < 3).astype(jnp.int32), jax.random.fold_in(arg_keys[8], 1), 0, 1)
    return {"layer_inputs": layer_inputs, "norm_gain": norm_gain, "value_weight": value_weight, "out_weight": out_weight, "scores": scores, "head_weight": head_weight, "lengths": lengths, "returns": returns, "response_mask": response_mask}


EPS = 1e-05

def attention_weights(logits, length_row):
    span_len = logits.shape[-1]
    query_place = lax.broadcasted_iota(jnp.int32, (span_len, span_len), 0)
    key_place = lax.broadcasted_iota(jnp.int32, (span_len, span_len), 1)
    allowed = (key_place <= query_place)[None, None] & (key_place[None, None] < length_row[:, None, None, None])
    masked = jnp.where(allowed, logits.astype(jnp.float32), -1e+30)
    row_top = lax.optimization_barrier(jnp.max(masked, axis=-1, keepdims=True))
    exponent = jnp.where(allowed, jnp.exp(masked - row_top), 0.0)
    return (exponent / lax.optimization_barrier(jnp.sum(exponent, axis=-1, keepdims=True))).astype(jnp.bfloat16)

def mix_values(attention, values):
    micro_count, head_count, span_len = attention.shape[:3]
    grouped = attention.astype(jnp.float32).reshape(micro_count, KVH, head_count // KVH, span_len, span_len)
    values_split = values.astype(jnp.float32).reshape(micro_count, span_len, KVH, HD)
    mixture = jnp.einsum('bgqij,bjgd->bigqd', grouped, values_split)
    return mixture.reshape(micro_count * span_len, head_count * HD).astype(jnp.bfloat16)

def unmix_grads(attention, grad_rows):
    micro_count, head_count, span_len = attention.shape[:3]
    grouped = attention.astype(jnp.float32).reshape(micro_count, KVH, head_count // KVH, span_len, span_len)
    grad_split = grad_rows.reshape(micro_count, span_len, KVH, head_count // KVH, HD)
    backward = jnp.einsum('bgqij,bigqd->bjgd', grouped, grad_split)
    return backward.reshape(micro_count * span_len, KVH * HD)

def reference(layer_inputs, norm_gain, value_weight, out_weight, scores, head_weight, lengths, returns, response_mask):
    token_index = jnp.arange(TOKENS, dtype=jnp.int32)
    length_flat = lengths.reshape(-1).astype(jnp.int32)
    block_len = length_flat[token_index // LMAX]
    live_mask = ((token_index % LMAX < block_len) & (response_mask == 1)).astype(jnp.float32)
    live_count = jnp.maximum(jnp.sum(live_mask), 1.0)
    return_mean = jnp.sum(live_mask * returns) / live_count
    return_var = jnp.sum(live_mask * (returns - return_mean) ** 2) / live_count
    target = (returns - return_mean) * lax.rsqrt(return_var + EPS)
    head_row = head_weight.astype(jnp.float32)
    grad_outs = []
    grad_values = []
    grad_gains = []
    upstream = None
    for section_index in range(SECTIONS - 1, -1, -1):
        layer_in = layer_inputs[section_index].astype(jnp.float32)
        gain_row = norm_gain[section_index]
        norm_scale = lax.rsqrt(lax.optimization_barrier(jnp.mean(layer_in * layer_in, axis=-1)) + EPS)
        normed = (layer_in * norm_scale[:, None] * gain_row).astype(jnp.bfloat16)
        value_sum = jnp.dot(normed, value_weight[section_index], preferred_element_type=jnp.float32)
        attention = attention_weights(scores[section_index].reshape(REPLICAS * MB, HEADS, LMAX, LMAX), length_flat)
        mixture = mix_values(attention, value_sum.astype(jnp.bfloat16))
        if section_index == SECTIONS - 1:
            hidden_out = layer_in + jnp.dot(mixture, out_weight[section_index], preferred_element_type=jnp.float32)
            out_scale = lax.rsqrt(lax.optimization_barrier(jnp.mean(hidden_out * hidden_out, axis=-1)) + EPS)
            critic_value = out_scale * lax.optimization_barrier(jnp.sum(hidden_out * head_row, axis=-1))
            value_error = live_mask * (critic_value - target)
            slope = out_scale[:, None] * head_row - (out_scale * out_scale * critic_value / D)[:, None] * hidden_out
            upstream = (value_error[:, None] * slope).astype(jnp.bfloat16)
        mixed_grad = jnp.dot(upstream, out_weight[section_index].T, preferred_element_type=jnp.float32)
        value_grad = unmix_grads(attention, mixed_grad).astype(jnp.bfloat16)
        normed_grad = jnp.dot(value_grad, value_weight[section_index].T, preferred_element_type=jnp.float32)
        inner_term = lax.optimization_barrier(jnp.sum(value_grad.astype(jnp.float32) * value_sum, axis=-1))
        input_grad = upstream.astype(jnp.float32) + norm_scale[:, None] * gain_row * normed_grad - (norm_scale * norm_scale * inner_term / D)[:, None] * layer_in
        grad_outs.append(jnp.dot(mixture.T, upstream, preferred_element_type=jnp.float32).astype(jnp.bfloat16))
        grad_values.append(jnp.dot(normed.T, value_grad, preferred_element_type=jnp.float32).astype(jnp.bfloat16))
        grad_gains.append(lax.optimization_barrier(jnp.sum(normed_grad * layer_in * norm_scale[:, None], axis=0)))
        upstream = input_grad.astype(jnp.bfloat16)
    return (jnp.stack(grad_outs[::-1]), jnp.stack(grad_values[::-1]), jnp.stack(grad_gains[::-1]))
```

```python
import jax
import jax.numpy as jnp
from jax import lax
from jax.experimental import pallas as pl
from jax.experimental.pallas import tpu as pltpu
from jax.sharding import PartitionSpec as P

D = 8192
HD = 128
KVH = 4
EPS = 1e-05
F32 = jnp.float32
BF16 = jnp.bfloat16
MESH = pl.DeviceIdType.MESH
COPIES = 200
ORDER = "mwmammammwamwgmbmgmwbmgbmgmgbmgbmggmmmmmmm"


def attention_weights(logits, length_row):
    span_len = logits.shape[-1]
    query_place = lax.broadcasted_iota(jnp.int32, (span_len, span_len), 0)
    key_place = lax.broadcasted_iota(jnp.int32, (span_len, span_len), 1)
    allowed = (key_place <= query_place)[None, None] & (
        key_place[None, None] < length_row[:, None, None, None]
    )
    masked = jnp.where(allowed, logits.astype(F32), -1e30)
    row_top = jnp.max(masked, axis=-1, keepdims=True)
    exponent = jnp.where(allowed, jnp.exp(masked - row_top), 0.0)
    return (exponent / jnp.sum(exponent, axis=-1, keepdims=True)).astype(BF16)


def dot(left, right):
    return jnp.dot(left, right, preferred_element_type=F32)


def split_pair(value):
    high = value.astype(BF16)
    return high, (value - high.astype(F32)).astype(BF16)


def kernel(
    att_ref, x_ref, gain_ref, wv_ref, w_ref, head_ref,
    go_ref, gv_ref, gg_ref,
    att_all, v_all, xf, part, sum1, r0, r1, r2, r2x, gr_all,
    sq, sq_in, bm, att_t, v_bd, up_bd, wb, wq, wvb, wvt, gains, rms_own, rms_all, hid, st, st_in,
    coef, ret, err_at, up, ng, vg, v_t, nrm_t, go_own, go_send, go_in, gv_own, gv_send, gv_in,
    gg_own, gg_send, gg_in,
    send_sems, recv_sems, local_sems,
):
    pipe = lax.axis_index("pipe")
    tensor = lax.axis_index("tensor")
    dp = lax.axis_index("dp")
    c = lax.rem(tensor, 2)
    xh = lax.div(tensor, 2)
    z = lax.div(dp, 4)
    y = lax.rem(dp, 4)
    a = jnp.where(c == 0, z, y)
    b = jnp.where(c == 0, y, z)
    other = 1 - pipe

    def dp_of(a_at, b_at):
        return jnp.where(c == 0, a_at * 4 + b_at, b_at * 4 + a_at)

    core_peer = {"tensor": xh * 2 + 1 - c}
    x_tensor = (1 - xh) * 2 + c
    x_peer = {"tensor": x_tensor}
    pipe_peer = {"pipe": other}
    a_next = [lax.rem(a + k, 4) for k in (1, 2, 3)]
    b_next = [lax.rem(b + k, 4) for k in (1, 2, 3)]
    a_peers = [{"dp": dp_of(at, b)} for at in a_next]
    ax_peers = [{"dp": dp_of(at, b), "tensor": x_tensor} for at in [a] + a_next]
    b_peers = [{"dp": dp_of(a, bt)} for bt in b_next]
    t_peers = [{"tensor": lax.rem(tensor + k, 4)} for k in (1, 2, 3)]
    dp_next = [lax.rem(dp + k, 16) for k in range(16)]
    used = [0]

    def remote(src, dst, device):
        at = used[0]
        used[0] += 1
        return pltpu.make_async_remote_copy(
            src_ref=src, dst_ref=dst, send_sem=send_sems.at[at], recv_sem=recv_sems.at[at],
            device_id=device, device_id_type=MESH,
        )

    def start(copies):
        for one in copies:
            one.start()
        return copies

    def finish(copies):
        for one in copies:
            one.wait()

    def rows_of(first, size):
        return pl.ds(pl.multiple_of(first, size), size)

    loads = [
        pltpu.make_async_copy(wv_ref, wvb.at[pipe], local_sems.at[0]),
        pltpu.make_async_copy(w_ref, wb.at[pipe], local_sems.at[1]),
    ]
    start(loads)
    barrier = pltpu.get_barrier_semaphore()
    partners = [{"dp": to} for to in dp_next[1:]] + t_peers + ax_peers[1:]
    partners += [{"dp": to, "pipe": other} for to in dp_next]
    partners += [{"tensor": one["tensor"], "pipe": other} for one in t_peers]
    for peer in partners:
        pl.semaphore_signal(barrier, inc=1, device_id=peer, device_id_type=MESH)
    pl.semaphore_wait(barrier, len(partners))

    def x_copy(to, device, half):
        return remote(
            x_ref.at[rows_of(half * 64, 64), rows_of(to * 128, 128)],
            xf.at[pipe, rows_of(dp * 64, 64)], device,
        )

    x_same = [x_copy(to, {"dp": to}, pipe) for to in dp_next[1:]]
    x_cross = [x_copy(to, {"dp": to, "pipe": other}, other) for to in dp_next]

    def send_x(layer):
        @pl.when(pipe == layer)
        def _():
            start(x_cross)
            start(x_same)
            xf[layer, rows_of(dp * 64, 64), :] = x_ref[rows_of(layer * 64, 64), rows_of(dp * 128, 128)]

    def wait_x(layer):
        @pl.when(pipe == layer)
        def _():
            finish(x_same)
            for one in x_cross:
                one.wait_send()

        @pl.when(pipe != layer)
        def _():
            for one in x_cross:
                one.wait_recv()

    att_cross = remote(att_ref.at[other], att_all.at[pipe, c, a, b, xh], pipe_peer)

    def gather_attention(layer):
        here = att_all.at[layer]

        @pl.when(pipe != layer)
        def _():
            att_cross.wait_recv()

        copies = start([remote(here.at[c, a, b, xh], here.at[c, a, b, xh], x_peer)])
        yield
        finish(copies)
        copies = start([remote(here.at[c, a, b], here.at[c, a, b], peer) for peer in a_peers])
        yield
        finish(copies)
        copies = start([remote(here.at[c, :, b], here.at[c, :, b], peer) for peer in b_peers])
        yield
        finish(copies)
        copies = start([remote(here.at[c], here.at[c], core_peer)])
        yield
        finish(copies)
        yield

    def scatter(layer, turn):
        here = part.at[turn]
        copies = start([remote(here.at[1 - c], r0.at[turn], core_peer)])
        yield
        finish(copies)

        def add0(at, carry):
            for bt in range(4):
                part[turn, c, at, bt] = (
                    part[turn, c, at, bt].astype(F32) + r0[turn, at, bt].astype(F32)
                ).astype(BF16)
            return carry

        lax.fori_loop(0, 4, add0, 0)
        copies = start([
            remote(here.at[c, :, bt], r1.at[turn, k], peer)
            for k, (bt, peer) in enumerate(zip(b_next, b_peers))
        ])
        yield
        finish(copies)
        for at in range(4):
            sum1[turn, at] = (
                part[turn, c, at, b].astype(F32) + r1[turn, 0, at].astype(F32)
                + r1[turn, 1, at].astype(F32) + r1[turn, 2, at].astype(F32)
            ).astype(BF16)
        copies = [
            remote(sum1.at[turn, at], r2x.at[turn, k], peer)
            for k, (at, peer) in enumerate(zip([a] + a_next, ax_peers))
        ]
        copies += [
            remote(sum1.at[turn, at], r2.at[turn, k], peer)
            for k, (at, peer) in enumerate(zip(a_next, a_peers))
        ]
        start(copies)
        yield
        finish(copies)

    def scattered(turn):
        total = sum1[turn, a].astype(F32)
        for k in range(3):
            total = total + r2[turn, k].astype(F32)
        for k in range(4):
            total = total + r2x[turn, k].astype(F32)
        return total

    def gather(here):
        copies = start([remote(here.at[c, a, b], here.at[c, a, b], peer) for peer in a_peers])
        yield
        finish(copies)
        copies = start([remote(here.at[c, :, b], here.at[c, :, b], peer) for peer in b_peers])
        yield
        finish(copies)
        copies = start([remote(here.at[c], here.at[c], core_peer)])
        yield
        finish(copies)

    head_row = head_ref[pl.ds(dp, 1), :]
    lane = lax.broadcasted_iota(jnp.int32, (128, 128), 1)

    def project(layer):
        gain_row = gains[layer, 0:1, :]

        def body(zi, carry):
            xg = (xf[layer, rows_of(zi * 256, 256), :].astype(F32) * gain_row).astype(BF16)
            out = dot(xg, wvb[layer]).astype(BF16)
            for yi in range(4):
                part[layer, 0, zi, yi] = out[yi * 64:yi * 64 + 32]
                part[layer, 1, yi, zi] = out[yi * 64 + 32:yi * 64 + 64]
            return carry

        lax.fori_loop(0, 4, body, 0)

    def forward(layer):
        wait_x(layer)
        project(layer)
        yield from scatter(layer, layer)
        rms = rms_own[layer, :, 0:1]
        total = scattered(layer) * rms
        high, low = split_pair(rms)
        place = lax.broadcasted_iota(jnp.int32, (32, 128), 1)
        extra = jnp.where(place == 0, high.astype(F32), jnp.where(place == 1, low.astype(F32), 0.0))
        v_all[layer, c, a, b, :, 0:512] = total.astype(BF16)
        v_all[layer, c, a, b, :, 512:640] = extra.astype(BF16)
        yield from gather(v_all.at[layer])

    def mixture():
        def body(zi, carry):
            for yi in range(4):
                first = pl.multiple_of(zi * 256 + yi * 64, 64)
                for g in range(4):
                    places = (0, zi, yi) if g % 2 == 0 else (1, yi, zi)
                    att = att_all[(1, *places, g // 2)][0:128, :]
                    cols = slice(g * 128, (g + 1) * 128)
                    for m in range(2):
                        values = v_all[(1, 0, zi, yi) if m == 0 else (1, 1, yi, zi)][:, cols]
                        for q in range(2):
                            at = q * 2 + m
                            v_bd[yi, g, at * 32:(at + 1) * 32, at * 128:(at + 1) * 128] = values
                    out = dot(att, v_bd[yi, g]).astype(BF16)
                    for h in range(4):
                        for q in range(2):
                            for m in range(2):
                                head = g * 8 + q * 4 + h
                                bm[1, pl.ds(first + m * 32, 32), head * 128:(head + 1) * 128] = (
                                    out[h * 32:(h + 1) * 32, (q * 2 + m) * 128:(q * 2 + m + 1) * 128]
                                )
            return carry

        lax.fori_loop(0, 4, body, 0)

    def out_project():
        def body(k, carry):
            rows = rows_of(k * 512, 512)
            hid[rows, :] = xf[1, rows, :].astype(F32) + dot(bm[1, rows, :], wb[1])
            return carry

        lax.fori_loop(0, 2, body, 0)
        tile = jnp.zeros((128, 128), F32)
        for k in range(8):
            h = hid[k * 128:(k + 1) * 128, :]
            tile = jnp.where(lane == k, jnp.sum(h * h, axis=1, keepdims=True), tile)
            tile = jnp.where(lane == 8 + k, jnp.sum(h * head_row, axis=1, keepdims=True), tile)
        st[0] = tile.T[0:16]

    def targets():
        for d in range(16):
            extra = att_all[1, 0, d // 4, d % 4, 0, 128:144, :].astype(F32)
            at = 8 * (d % 2) + d // 2
            ret[at:at + 1, :] = extra[0:1] + extra[1:2] + extra[2:3]
            ret[16 + at:17 + at, :] = extra[3:4]
        returns = ret[0:16, :]
        live = ret[16:32, :]

        def whole(value):
            return jnp.sum(jnp.sum(value, axis=1, keepdims=True), axis=0, keepdims=True)

        count = jnp.maximum(whole(live), 1.0)
        mean = whole(live * returns) / count
        spread = whole(live * (returns - mean) * (returns - mean)) / count
        target = (returns - mean) * lax.rsqrt(spread + EPS)
        low = lax.broadcasted_iota(jnp.int32, (8, 128), 1) < 64
        for at, value in enumerate((target, live)):
            even, odd = value[0:8], value[8:16]
            err_at[0, at] = jnp.where(low, even, pltpu.roll(odd, 64, 1))
            err_at[1, at] = jnp.where(low, pltpu.roll(even, 64, 1), odd)

    def upstream(sums):
        target, live = err_at[pipe, 0], err_at[pipe, 1]
        out_scale = lax.rsqrt(sums[0:8] / D + EPS)
        critic = out_scale * sums[8:16]
        alpha = live * (critic - target) * out_scale
        beta = alpha * out_scale * critic / D
        coef[...] = jnp.concatenate([alpha, beta, jnp.zeros((112, 128), F32)], axis=0).T
        for k in range(8):
            rows = slice(k * 128, (k + 1) * 128)
            up[1, rows, :] = (
                coef[:, k:k + 1] * head_row - coef[:, 8 + k:9 + k] * hid[rows, :]
            ).astype(BF16)

    def turn_attention(layer):
        def body(zi, carry):
            for yi in range(4):
                for g in range(4):
                    places = (0, zi, yi) if g % 2 == 0 else (1, yi, zi)
                    turned = att_all[(layer, *places, g // 2)][0:128, :].T
                    for q in range(2):
                        for m in range(2):
                            att_t[layer, zi * 4 + yi, m, (g * 2 + q) * 32:(g * 2 + q + 1) * 32, :] = (
                                turned[(q * 2 + m) * 32:(q * 2 + m + 1) * 32]
                            )
            return carry

        lax.fori_loop(0, 4, body, 0)

    def prepare(layer):
        gain_row = gains[layer, 0:1, :]

        def body(zi, carry):
            for pair in range(2):
                first = pl.multiple_of(zi * 256 + pair * 128, 128)
                packets = []
                for yi in (pair * 2, pair * 2 + 1):
                    packets.append(v_all.at[layer, 0, zi, yi])
                    packets.append(v_all.at[layer, 1, yi, zi])
                extra = jnp.concatenate([one[:, 512:640] for one in packets], axis=0).astype(F32)
                rms = extra[:, 0:1] + extra[:, 1:2]
                rms_all[layer, pl.ds(first, 128), :] = jnp.broadcast_to(rms, (128, 128))
                normed = xf[layer, pl.ds(first, 128), :].astype(F32) * rms * gain_row
                nrm_t[layer, :, pl.ds(first, 128)] = normed.astype(BF16).T
                for g in range(4):
                    cols = slice(g * 128, (g + 1) * 128)
                    values = jnp.concatenate([one[:, cols] for one in packets], axis=0)
                    v_t[layer, g, :, pl.ds(first, 128)] = values.T
            return carry

        lax.fori_loop(0, 4, body, 0)

    def unmix(layer):
        def spread(d, carry):
            for m in range(2):
                first = pl.multiple_of(d * 64 + m * 32, 32)
                rows = up[layer, pl.ds(first, 32), :]
                for h in range(4):
                    up_bd[m, h * 32:(h + 1) * 32, h * 128:(h + 1) * 128] = rows
                out = dot(att_t[layer, d, m], up_bd[m]).astype(BF16)
                for q in range(8):
                    bm[layer, pl.ds(first, 32), q * 512:(q + 1) * 512] = out[q * 32:(q + 1) * 32, :]
            return carry

        lax.fori_loop(0, 16, spread, 0)

        def body(k, carry):
            rows = rows_of(k * 512, 512)
            for g in range(4):
                cols = slice(g * 1024, (g + 1) * 1024)
                out = dot(bm[layer, rows, cols], wq[layer, cols, :]).astype(BF16)
                for zi in range(2):
                    for yi in range(4):
                        first = zi * 256 + yi * 64
                        into = slice(g * 128, (g + 1) * 128)
                        part[2 + layer, 0, k * 2 + zi, yi, :, into] = out[first:first + 32]
                        part[2 + layer, 1, yi, k * 2 + zi, :, into] = out[first + 32:first + 64]
            return carry

        lax.fori_loop(0, 2, body, 0)

    def norm_back(layer):
        def body(zi, carry):
            first = pl.multiple_of(zi * 256, 256)
            for yi in range(4):
                vg[layer, pl.ds(first + yi * 64, 32), :] = gr_all[layer, 0, zi, yi]
                vg[layer, pl.ds(first + yi * 64 + 32, 32), :] = gr_all[layer, 1, yi, zi]
            ng[layer, pl.ds(first, 256), :] = dot(vg[layer, pl.ds(first, 256), :], wvt[layer])
            return carry

        lax.fori_loop(0, 4, body, 0)

    def input_grad(layer):
        gain_row = gains[layer, 0:1, :]

        def body(zi, carry):
            for yi in range(4):
                for m in range(2):
                    rows = pl.ds(pl.multiple_of(zi * 256 + yi * 64 + m * 32, 32), 32)
                    values = v_all[(layer, 0, zi, yi) if m == 0 else (layer, 1, yi, zi)][:, 0:512]
                    product = vg[layer, rows, :].astype(F32) * values.astype(F32)
                    inner = jnp.sum(product, axis=1, keepdims=True)
                    rms = rms_all[layer, rows, :]
                    up[layer - 1, rows, :] = (
                        up[layer, rows, :].astype(F32) + rms * gain_row * ng[layer, rows, :]
                        - (rms * rms * (inner / D)) * xf[layer, rows, :].astype(F32)
                    ).astype(BF16)
            return carry

        lax.fori_loop(0, 4, body, 0)

    go_copies = [
        remote(go_send.at[k * 1024:(k + 1) * 1024], go_in.at[k * 1024:(k + 1) * 1024], pipe_peer)
        for k in range(4)
    ]
    gv_copy = remote(gv_send, gv_in, pipe_peer)
    gg_copy = remote(gg_send, gg_in, pipe_peer)

    def out_grad(layer):
        for g in range(4):
            def body(k, carry):
                out = dot(v_t[layer, g], bm[layer, :, rows_of(g * 1024 + k * 512, 512)])

                @pl.when(pipe == layer)
                def _():
                    for h in range(4):
                        go_own[rows_of(g * 1024 + k * 512 + h * 128, 128), :] = (
                            out[:, h * 128:(h + 1) * 128]
                        )

                @pl.when(pipe != layer)
                def _():
                    for h in range(4):
                        go_send[rows_of(g * 1024 + k * 512 + h * 128, 128), :] = (
                            out[:, h * 128:(h + 1) * 128].astype(BF16)
                        )

                return carry

            lax.fori_loop(0, 2, body, 0)

            @pl.when(pipe != layer)
            def _():
                go_copies[g].start()

    def small_grads(layer):
        def value_grad(k, total):
            cols = rows_of(k * 256, 256)
            return total + dot(nrm_t[layer, :, cols], vg[layer, cols, :])

        value_total = lax.fori_loop(0, 4, value_grad, jnp.zeros((128, 512), F32))

        def gain_grad(k, total):
            rows = rows_of(k * 128, 128)
            gained = ng[layer, rows, :] * xf[layer, rows, :].astype(F32) * rms_all[layer, rows, :]
            return total + jnp.sum(gained.reshape(16, 8, 128), axis=0)

        gain_total = lax.fori_loop(0, 8, gain_grad, jnp.zeros((8, 128), F32))

        @pl.when(pipe == layer)
        def _():
            gv_own[...] = value_total
            gg_own[...] = gain_total

        @pl.when(pipe != layer)
        def _():
            gv_send[...] = value_total.astype(BF16)
            gg_send[...] = gain_total
            gv_copy.start()
            gg_copy.start()

    def sum_up(copies, peers, at):
        for one in copies:
            one.wait()
        st[at + 1] = st[at] + st_in[at, 0] + st_in[at, 1] + st_in[at, 2]

    def main():
        yield from forward(1)
        mixture()
        out_project()
        copies = start([remote(st.at[0], st_in.at[0, k], peer) for k, peer in enumerate(t_peers)])
        yield
        turn_attention(1)
        targets()
        sum_up(copies, t_peers, 0)
        copies = start([remote(st.at[1], st_in.at[1, k], peer) for k, peer in enumerate(b_peers)])
        yield
        prepare(1)
        sum_up(copies, b_peers, 1)
        copies = start([remote(st.at[2], st_in.at[2, k], peer) for k, peer in enumerate(a_peers)])
        yield
        sum_up(copies, a_peers, 2)
        upstream(st[3])
        for layer in (1, 0):
            unmix(layer)
            turn = 2 + layer
            steps = scatter(layer, turn)
            next(steps)
            yield
            next(steps)
            out_grad(layer)
            yield
            yield from steps
            gr_all[layer, c, a, b] = scattered(turn).astype(BF16)
            steps = gather(gr_all.at[layer])
            next(steps)
            yield
            next(steps)
            if layer == 0:
                small_grads(1)
            yield
            yield from steps
            norm_back(layer)
            if layer == 1:
                input_grad(1)
        small_grads(0)
        yield

    def background():
        yield from forward(0)
        turn_attention(0)
        yield
        prepare(0)
        yield

    gains[pipe, 0:8, :] = jnp.broadcast_to(gain_ref[pl.ds(dp, 1), :], (8, 128))
    loads[0].wait()
    cross = [
        remote(gains.at[pipe], gains.at[pipe], pipe_peer),
        remote(wvb.at[pipe], wvb.at[pipe], pipe_peer),
    ]
    send_x(1)
    start(cross)
    att_cross.start()
    att_all[pipe, c, a, b, xh] = att_ref[pipe]
    for m in range(4):
        rows = x_ref[m * 32:(m + 1) * 32, :].astype(F32)
        sq[m] = jnp.broadcast_to(jnp.sum(rows * rows, axis=1, keepdims=True), (32, 128))
    sq_in[pipe, tensor] = sq[pipe * 2 + c]
    squares = []
    for peer in t_peers:
        own = lax.rem(peer["tensor"], 2)
        squares.append(remote(sq.at[pipe * 2 + own], sq_in.at[pipe, tensor], peer))
        squares.append(remote(
            sq.at[other * 2 + own], sq_in.at[pipe, tensor], {"tensor": peer["tensor"], "pipe": other}
        ))
    squares.append(remote(sq.at[other * 2 + c], sq_in.at[pipe, tensor], pipe_peer))
    start(squares)
    attention1 = gather_attention(1)
    next(attention1)
    loads[1].wait()

    def turn_w(layer):
        def body(k, carry):
            wq[layer, rows_of(k * 128, 128), :] = wb[layer, rows_of(k * 128, 128), :].T
            return carry

        lax.fori_loop(0, 32, body, 0)
        for k in range(4):
            wvt[layer, k * 128:(k + 1) * 128, :] = wvb[layer, :, k * 128:(k + 1) * 128].T

    v_bd[...] = jnp.zeros_like(v_bd)
    up_bd[...] = jnp.zeros_like(up_bd)
    finish(squares)
    for layer in range(2):
        squared = sq_in[layer, 0] + sq_in[layer, 1] + sq_in[layer, 2] + sq_in[layer, 3]
        rms_own[layer] = lax.rsqrt(squared / D + EPS)
    finish(cross)
    next(attention1)

    @pl.when(pipe == 1)
    def _():
        att_cross.wait_send()

    w_cross = remote(wb.at[pipe], wb.at[pipe], pipe_peer)

    def weights():
        w_cross.start()
        send_x(0)
        yield
        w_cross.wait()
        yield
        turn_w(1)
        yield
        turn_w(0)
        yield

    streams = {
        "m": main(), "g": background(), "a": attention1, "b": gather_attention(0), "w": weights(),
    }
    for name in ORDER:
        next(streams[name])

    @pl.when(pipe == 0)
    def _():
        att_cross.wait_send()

    def add_halves(k, carry):
        rows = rows_of(k * 256, 256)
        go_ref[rows, :] = (go_own[rows, :] + go_in[rows, :].astype(F32)).astype(BF16)
        return carry

    for one in go_copies:
        one.wait()
    lax.fori_loop(0, 16, add_halves, 0)
    gv_copy.wait()
    gg_copy.wait()
    gv_ref[...] = (gv_own[...] + gv_in[...].astype(F32)).astype(BF16)
    gg_ref[...] = jnp.sum(gg_own[...] + gg_in[...], axis=0, keepdims=True)


def shards(
    layer_inputs, norm_gain, value_weight, out_weight, scores, head_weight, lengths, returns,
    response_mask,
):
    replica = lax.axis_index("dp")
    own_lengths = lax.dynamic_index_in_dim(lengths, replica, 0, keepdims=False)
    attention = attention_weights(scores[0, 0], own_lengths)
    packed = attention.reshape(2, 2, 2, 4, 32, 32).transpose(0, 3, 4, 2, 1, 5).reshape(2, 128, 128)
    position = jnp.arange(128, dtype=jnp.int32)
    block_len = jnp.repeat(own_lengths, 32, total_repeat_length=128)
    live = ((position % 32 < block_len) & (response_mask == 1)).astype(F32)
    high = returns.astype(BF16)
    rest = returns - high.astype(F32)
    middle = rest.astype(BF16)
    low = (rest - middle.astype(F32)).astype(BF16)
    extra = jnp.stack([high, middle, low, live.astype(BF16)])
    extra = jnp.concatenate([extra, jnp.zeros((12, 128), BF16)], axis=0)
    packet = jnp.concatenate([packed, jnp.broadcast_to(extra, (2, 16, 128))], axis=1)

    vmem = pl.BlockSpec(memory_space=pltpu.VMEM)
    anywhere = pl.BlockSpec(memory_space=pl.ANY)

    def scratch(*shape, dtype=BF16):
        return pltpu.VMEM(shape, dtype)

    grad_out, grad_value, grad_gain = pl.pallas_call(
        kernel,
        out_shape=(
            jax.ShapeDtypeStruct((4096, 128), BF16),
            jax.ShapeDtypeStruct((128, 512), BF16),
            jax.ShapeDtypeStruct((1, 128), F32),
        ),
        in_specs=[vmem, vmem, vmem, anywhere, anywhere, vmem],
        out_specs=(vmem, vmem, vmem),
        scratch_shapes=[
            scratch(2, 2, 4, 4, 2, 144, 128),
            scratch(2, 2, 4, 4, 32, 640),
            scratch(2, 1024, 128),
            scratch(4, 2, 4, 4, 32, 512),
            scratch(4, 4, 32, 512),
            scratch(4, 4, 4, 32, 512),
            scratch(4, 3, 4, 32, 512),
            scratch(4, 3, 32, 512),
            scratch(4, 4, 32, 512),
            scratch(2, 2, 4, 4, 32, 512),
            scratch(4, 32, 128, dtype=F32),
            scratch(2, 4, 32, 128, dtype=F32),
            scratch(2, 1024, 4096),
            scratch(2, 16, 2, 256, 128),
            scratch(4, 4, 128, 512),
            scratch(2, 128, 512),
            scratch(2, 4096, 128),
            scratch(2, 4096, 128),
            scratch(2, 128, 512),
            scratch(2, 512, 128),
            scratch(2, 8, 128, dtype=F32),
            scratch(2, 32, 128, dtype=F32),
            scratch(2, 1024, 128, dtype=F32),
            scratch(1024, 128, dtype=F32),
            scratch(4, 16, 128, dtype=F32),
            scratch(3, 3, 16, 128, dtype=F32),
            scratch(128, 128, dtype=F32),
            scratch(32, 128, dtype=F32),
            scratch(2, 2, 8, 128, dtype=F32),
            scratch(2, 1024, 128),
            scratch(2, 1024, 128, dtype=F32),
            scratch(2, 1024, 512),
            scratch(2, 4, 128, 1024),
            scratch(2, 128, 1024),
            scratch(4096, 128, dtype=F32),
            scratch(4096, 128),
            scratch(4096, 128),
            scratch(128, 512, dtype=F32),
            scratch(128, 512),
            scratch(128, 512),
            scratch(8, 128, dtype=F32),
            scratch(8, 128, dtype=F32),
            scratch(8, 128, dtype=F32),
            pltpu.SemaphoreType.DMA((COPIES,)),
            pltpu.SemaphoreType.DMA((COPIES,)),
            pltpu.SemaphoreType.DMA((2,)),
        ],
        compiler_params=pltpu.CompilerParams(
            collective_id=0, has_side_effects=True, vmem_limit_bytes=60 * 1024 * 1024
        ),
        cost_estimate=pl.CostEstimate(
            flops=8_000_000_000, bytes_accessed=6_000_000, transcendentals=0
        ),
    )(
        packet,
        layer_inputs[0],
        norm_gain[0].reshape(16, 128),
        value_weight[0],
        out_weight[0],
        head_weight.astype(F32).reshape(16, 128),
    )
    return grad_out[None], grad_value[None], grad_gain


def solution(mesh):
    return jax.shard_map(
        shards,
        mesh=mesh,
        in_specs=(
            P("pipe", "dp", "tensor"),
            P("pipe", "tensor"),
            P("pipe", ("tensor", "dp"), None),
            P("pipe", None, ("tensor", "dp")),
            P("pipe", "dp", None, "tensor", None, None),
            P("tensor"),
            P(),
            P("dp"),
            P("dp"),
        ),
        out_specs=(
            P("pipe", None, ("tensor", "dp")),
            P("pipe", ("tensor", "dp"), None),
            P("pipe", ("tensor", "dp")),
        ),
        check_vma=False,
    )
```

```python
import jax
import jax.numpy as jnp
from jax import lax
from jax.experimental import pallas as pl
from jax.experimental.pallas import tpu as pltpu
from jax.sharding import PartitionSpec as P

D = 8192
HD = 128
KVH = 4
EPS = 1e-05
F32 = jnp.float32
BF16 = jnp.bfloat16
MESH = pl.DeviceIdType.MESH
COPIES = 200
ORDER = "mwmawwmmawmwwmawsmwwmwmbuumuugmuubugmugmbgmubgmoogmbougmgoomooqqqmmoqmqqmqqm"


def attention_weights(logits, length_row):
    span_len = logits.shape[-1]
    query_place = lax.broadcasted_iota(jnp.int32, (span_len, span_len), 0)
    key_place = lax.broadcasted_iota(jnp.int32, (span_len, span_len), 1)
    allowed = (key_place <= query_place)[None, None] & (
        key_place[None, None] < length_row[:, None, None, None]
    )
    masked = jnp.where(allowed, logits.astype(F32), -1e30)
    row_top = jnp.max(masked, axis=-1, keepdims=True)
    exponent = jnp.where(allowed, jnp.exp(masked - row_top), 0.0)
    return (exponent / jnp.sum(exponent, axis=-1, keepdims=True)).astype(BF16)


def dot(left, right):
    return jnp.dot(left, right, preferred_element_type=F32)


def split_pair(value):
    high = value.astype(BF16)
    return high, (value - high.astype(F32)).astype(BF16)


def kernel(
    att_ref, x_ref, gain_ref, wv_ref, w_ref, head_ref,
    go_ref, gv_ref, gg_ref,
    att_all, v_all, xf, part, sum1, r0, r1, r2, r2x, gr_all,
    sq, sq_in, bm, att_t, v_bd, up_bd, wb, wq, wvb, wvt, gains, rms_own, rms_all, hid, st, st_in,
    coef, ret, err_at, up, ng, vg, v_t, nrm_t, go_own, go_send, go_in, gv_own, gv_send, gv_in,
    gg_own, gg_send, gg_in,
    send_sems, recv_sems, local_sems,
):
    pipe = lax.axis_index("pipe")
    tensor = lax.axis_index("tensor")
    dp = lax.axis_index("dp")
    c = lax.rem(tensor, 2)
    xh = lax.div(tensor, 2)
    z = lax.div(dp, 4)
    y = lax.rem(dp, 4)
    a = jnp.where(c == 0, z, y)
    b = jnp.where(c == 0, y, z)
    other = 1 - pipe

    def dp_of(a_at, b_at):
        return jnp.where(c == 0, a_at * 4 + b_at, b_at * 4 + a_at)

    core_peer = {"tensor": xh * 2 + 1 - c}
    x_tensor = (1 - xh) * 2 + c
    x_peer = {"tensor": x_tensor}
    pipe_peer = {"pipe": other}
    a_next = [lax.rem(a + k, 4) for k in (1, 2, 3)]
    b_next = [lax.rem(b + k, 4) for k in (1, 2, 3)]
    a_peers = [{"dp": dp_of(at, b)} for at in a_next]
    ax_peers = [{"dp": dp_of(at, b), "tensor": x_tensor} for at in [a] + a_next]
    b_peers = [{"dp": dp_of(a, bt)} for bt in b_next]
    t_peers = [{"tensor": lax.rem(tensor + k, 4)} for k in (1, 2, 3)]
    dp_next = [lax.rem(dp + k, 16) for k in range(16)]
    used = [0]

    def remote(src, dst, device):
        at = used[0]
        used[0] += 1
        return pltpu.make_async_remote_copy(
            src_ref=src, dst_ref=dst, send_sem=send_sems.at[at], recv_sem=recv_sems.at[at],
            device_id=device, device_id_type=MESH,
        )

    def start(copies):
        for one in copies:
            one.start()
        return copies

    def finish(copies):
        for one in copies:
            one.wait()

    def rows_of(first, size):
        return pl.ds(pl.multiple_of(first, size), size)

    loads = [
        pltpu.make_async_copy(wv_ref, wvb.at[pipe], local_sems.at[0]),
        pltpu.make_async_copy(w_ref, wb.at[pipe], local_sems.at[1]),
    ]
    start(loads)
    barrier = pltpu.get_barrier_semaphore()
    partners = [{"dp": to} for to in dp_next[1:]] + t_peers + ax_peers[1:]
    partners += [{"dp": to, "pipe": other} for to in dp_next]
    partners += [{"tensor": one["tensor"], "pipe": other} for one in t_peers]
    for peer in partners:
        pl.semaphore_signal(barrier, inc=1, device_id=peer, device_id_type=MESH)
    pl.semaphore_wait(barrier, len(partners))

    def x_copy(to, device, half):
        return remote(
            x_ref.at[rows_of(half * 64, 64), rows_of(to * 128, 128)],
            xf.at[pipe, rows_of(dp * 64, 64)], device,
        )

    x_same = [x_copy(to, {"dp": to}, pipe) for to in dp_next[1:]]
    x_cross = [x_copy(to, {"dp": to, "pipe": other}, other) for to in dp_next]

    def send_x(layer):
        @pl.when(pipe == layer)
        def _():
            start(x_cross)
            start(x_same)
            xf[layer, rows_of(dp * 64, 64), :] = x_ref[rows_of(layer * 64, 64), rows_of(dp * 128, 128)]

    def wait_x(layer):
        @pl.when(pipe == layer)
        def _():
            finish(x_same)
            for one in x_cross:
                one.wait_send()

        @pl.when(pipe != layer)
        def _():
            for one in x_cross:
                one.wait_recv()

    att_cross = remote(att_ref.at[other], att_all.at[pipe, c, a, b, xh], pipe_peer)

    def gather_attention(layer):
        here = att_all.at[layer]

        @pl.when(pipe != layer)
        def _():
            att_cross.wait_recv()

        copies = start([remote(here.at[c, a, b, xh], here.at[c, a, b, xh], x_peer)])
        yield
        finish(copies)
        copies = start([remote(here.at[c, a, b], here.at[c, a, b], peer) for peer in a_peers])
        yield
        finish(copies)
        copies = start([remote(here.at[c, :, b], here.at[c, :, b], peer) for peer in b_peers])
        yield
        finish(copies)
        copies = start([remote(here.at[c], here.at[c], core_peer)])
        yield
        finish(copies)
        yield

    def scatter(layer, turn):
        here = part.at[turn]
        copies = start([remote(here.at[1 - c], r0.at[turn], core_peer)])
        yield
        finish(copies)

        def add0(at, carry):
            for bt in range(4):
                part[turn, c, at, bt] = (
                    part[turn, c, at, bt].astype(F32) + r0[turn, at, bt].astype(F32)
                ).astype(BF16)
            return carry

        lax.fori_loop(0, 4, add0, 0)
        copies = start([
            remote(here.at[c, :, bt], r1.at[turn, k], peer)
            for k, (bt, peer) in enumerate(zip(b_next, b_peers))
        ])
        yield
        finish(copies)
        for at in range(4):
            sum1[turn, at] = (
                part[turn, c, at, b].astype(F32) + r1[turn, 0, at].astype(F32)
                + r1[turn, 1, at].astype(F32) + r1[turn, 2, at].astype(F32)
            ).astype(BF16)
        copies = [
            remote(sum1.at[turn, at], r2x.at[turn, k], peer)
            for k, (at, peer) in enumerate(zip([a] + a_next, ax_peers))
        ]
        copies += [
            remote(sum1.at[turn, at], r2.at[turn, k], peer)
            for k, (at, peer) in enumerate(zip(a_next, a_peers))
        ]
        start(copies)
        yield
        finish(copies)

    def scattered(turn):
        total = sum1[turn, a].astype(F32)
        for k in range(3):
            total = total + r2[turn, k].astype(F32)
        for k in range(4):
            total = total + r2x[turn, k].astype(F32)
        return total

    def gather(here):
        copies = start([remote(here.at[c, a, b], here.at[c, a, b], peer) for peer in a_peers])
        yield
        finish(copies)
        copies = start([remote(here.at[c, :, b], here.at[c, :, b], peer) for peer in b_peers])
        yield
        finish(copies)
        copies = start([remote(here.at[c], here.at[c], core_peer)])
        yield
        finish(copies)

    head_row = head_ref[pl.ds(dp, 1), :]
    lane = lax.broadcasted_iota(jnp.int32, (128, 128), 1)

    def project(layer):
        gain_row = gains[layer, 0:1, :]

        def body(zi, carry):
            xg = (xf[layer, rows_of(zi * 256, 256), :].astype(F32) * gain_row).astype(BF16)
            out = dot(xg, wvb[layer]).astype(BF16)
            for yi in range(4):
                part[layer, 0, zi, yi] = out[yi * 64:yi * 64 + 32]
                part[layer, 1, yi, zi] = out[yi * 64 + 32:yi * 64 + 64]
            return carry

        lax.fori_loop(0, 4, body, 0)

    def forward(layer):
        wait_x(layer)
        project(layer)
        yield from scatter(layer, layer)
        rms = rms_own[layer, :, 0:1]
        total = scattered(layer) * rms
        high, low = split_pair(rms)
        place = lax.broadcasted_iota(jnp.int32, (32, 128), 1)
        extra = jnp.where(place == 0, high.astype(F32), jnp.where(place == 1, low.astype(F32), 0.0))
        v_all[layer, c, a, b, :, 0:512] = total.astype(BF16)
        v_all[layer, c, a, b, :, 512:640] = extra.astype(BF16)
        yield from gather(v_all.at[layer])

    def mixture():
        def body(zi, carry):
            for yi in range(4):
                first = pl.multiple_of(zi * 256 + yi * 64, 64)
                for g in range(4):
                    places = (0, zi, yi) if g % 2 == 0 else (1, yi, zi)
                    att = att_all[(1, *places, g // 2)][0:128, :]
                    cols = slice(g * 128, (g + 1) * 128)
                    for m in range(2):
                        values = v_all[(1, 0, zi, yi) if m == 0 else (1, 1, yi, zi)][:, cols]
                        for q in range(2):
                            at = q * 2 + m
                            v_bd[yi, g, at * 32:(at + 1) * 32, at * 128:(at + 1) * 128] = values
                    out = dot(att, v_bd[yi, g]).astype(BF16)
                    for h in range(4):
                        for q in range(2):
                            for m in range(2):
                                head = g * 8 + q * 4 + h
                                bm[1, pl.ds(first + m * 32, 32), head * 128:(head + 1) * 128] = (
                                    out[h * 32:(h + 1) * 32, (q * 2 + m) * 128:(q * 2 + m + 1) * 128]
                                )
            return carry

        lax.fori_loop(0, 4, body, 0)

    def out_project():
        def body(k, carry):
            rows = rows_of(k * 512, 512)
            hid[rows, :] = xf[1, rows, :].astype(F32) + dot(bm[1, rows, :], wb[1])
            return carry

        lax.fori_loop(0, 2, body, 0)
        tile = jnp.zeros((128, 128), F32)
        for k in range(8):
            h = hid[k * 128:(k + 1) * 128, :]
            tile = jnp.where(lane == k, jnp.sum(h * h, axis=1, keepdims=True), tile)
            tile = jnp.where(lane == 8 + k, jnp.sum(h * head_row, axis=1, keepdims=True), tile)
        st[0] = tile.T[0:16]

    def targets():
        for d in range(16):
            extra = att_all[1, 0, d // 4, d % 4, 0, 128:144, :].astype(F32)
            at = 8 * (d % 2) + d // 2
            ret[at:at + 1, :] = extra[0:1] + extra[1:2] + extra[2:3]
            ret[16 + at:17 + at, :] = extra[3:4]
        returns = ret[0:16, :]
        live = ret[16:32, :]

        def whole(value):
            return jnp.sum(jnp.sum(value, axis=1, keepdims=True), axis=0, keepdims=True)

        count = jnp.maximum(whole(live), 1.0)
        mean = whole(live * returns) / count
        spread = whole(live * (returns - mean) * (returns - mean)) / count
        target = (returns - mean) * lax.rsqrt(spread + EPS)
        low = lax.broadcasted_iota(jnp.int32, (8, 128), 1) < 64
        for at, value in enumerate((target, live)):
            even, odd = value[0:8], value[8:16]
            err_at[0, at] = jnp.where(low, even, pltpu.roll(odd, 64, 1))
            err_at[1, at] = jnp.where(low, pltpu.roll(even, 64, 1), odd)

    def upstream(sums):
        target, live = err_at[pipe, 0], err_at[pipe, 1]
        out_scale = lax.rsqrt(sums[0:8] / D + EPS)
        critic = out_scale * sums[8:16]
        alpha = live * (critic - target) * out_scale
        beta = alpha * out_scale * critic / D
        coef[...] = jnp.concatenate([alpha, beta, jnp.zeros((112, 128), F32)], axis=0).T
        for k in range(8):
            rows = slice(k * 128, (k + 1) * 128)
            up[1, rows, :] = (
                coef[:, k:k + 1] * head_row - coef[:, 8 + k:9 + k] * hid[rows, :]
            ).astype(BF16)

    def turn_attention(layer):
        def body(zi, carry):
            for yi in range(4):
                for g in range(4):
                    places = (0, zi, yi) if g % 2 == 0 else (1, yi, zi)
                    turned = att_all[(layer, *places, g // 2)][0:128, :].T
                    for q in range(2):
                        for m in range(2):
                            att_t[layer, zi * 4 + yi, m, (g * 2 + q) * 32:(g * 2 + q + 1) * 32, :] = (
                                turned[(q * 2 + m) * 32:(q * 2 + m + 1) * 32]
                            )
            return carry

        lax.fori_loop(0, 4, body, 0)

    def prepare(layer):
        gain_row = gains[layer, 0:1, :]

        def body(zi, carry):
            for pair in range(2):
                first = pl.multiple_of(zi * 256 + pair * 128, 128)
                packets = []
                for yi in (pair * 2, pair * 2 + 1):
                    packets.append(v_all.at[layer, 0, zi, yi])
                    packets.append(v_all.at[layer, 1, yi, zi])
                extra = jnp.concatenate([one[:, 512:640] for one in packets], axis=0).astype(F32)
                rms = extra[:, 0:1] + extra[:, 1:2]
                rms_all[layer, pl.ds(first, 128), :] = jnp.broadcast_to(rms, (128, 128))
                normed = xf[layer, pl.ds(first, 128), :].astype(F32) * rms * gain_row
                nrm_t[layer, :, pl.ds(first, 128)] = normed.astype(BF16).T
                for g in range(4):
                    cols = slice(g * 128, (g + 1) * 128)
                    values = jnp.concatenate([one[:, cols] for one in packets], axis=0)
                    v_t[layer, g, :, pl.ds(first, 128)] = values.T
            return carry

        lax.fori_loop(0, 4, body, 0)

    def unmix(layer):
        def spread(d, carry):
            for m in range(2):
                first = pl.multiple_of(d * 64 + m * 32, 32)
                rows = up[layer, pl.ds(first, 32), :]
                for h in range(4):
                    up_bd[m, h * 32:(h + 1) * 32, h * 128:(h + 1) * 128] = rows
                out = dot(att_t[layer, d, m], up_bd[m]).astype(BF16)
                for q in range(8):
                    bm[layer, pl.ds(first, 32), q * 512:(q + 1) * 512] = out[q * 32:(q + 1) * 32, :]
            return carry

        lax.fori_loop(0, 16, spread, 0)

        def body(k, carry):
            rows = rows_of(k * 512, 512)
            for g in range(4):
                cols = slice(g * 1024, (g + 1) * 1024)
                out = dot(bm[layer, rows, cols], wq[layer, cols, :]).astype(BF16)
                for zi in range(2):
                    for yi in range(4):
                        first = zi * 256 + yi * 64
                        into = slice(g * 128, (g + 1) * 128)
                        part[2 + layer, 0, k * 2 + zi, yi, :, into] = out[first:first + 32]
                        part[2 + layer, 1, yi, k * 2 + zi, :, into] = out[first + 32:first + 64]
            return carry

        lax.fori_loop(0, 2, body, 0)

    def norm_back(layer):
        def body(zi, carry):
            first = pl.multiple_of(zi * 256, 256)
            for yi in range(4):
                vg[layer, pl.ds(first + yi * 64, 32), :] = gr_all[layer, 0, zi, yi]
                vg[layer, pl.ds(first + yi * 64 + 32, 32), :] = gr_all[layer, 1, yi, zi]
            ng[layer, pl.ds(first, 256), :] = dot(vg[layer, pl.ds(first, 256), :], wvt[layer])
            return carry

        lax.fori_loop(0, 4, body, 0)

    def input_grad(layer):
        gain_row = gains[layer, 0:1, :]

        def body(zi, carry):
            for yi in range(4):
                for m in range(2):
                    rows = pl.ds(pl.multiple_of(zi * 256 + yi * 64 + m * 32, 32), 32)
                    values = v_all[(layer, 0, zi, yi) if m == 0 else (layer, 1, yi, zi)][:, 0:512]
                    product = vg[layer, rows, :].astype(F32) * values.astype(F32)
                    inner = jnp.sum(product, axis=1, keepdims=True)
                    rms = rms_all[layer, rows, :]
                    up[layer - 1, rows, :] = (
                        up[layer, rows, :].astype(F32) + rms * gain_row * ng[layer, rows, :]
                        - (rms * rms * (inner / D)) * xf[layer, rows, :].astype(F32)
                    ).astype(BF16)
            return carry

        lax.fori_loop(0, 4, body, 0)

    go_copies = [
        remote(go_send.at[k * 512:(k + 1) * 512], go_in.at[k * 512:(k + 1) * 512], pipe_peer)
        for k in range(8)
    ]
    gv_copy = remote(gv_send, gv_in, pipe_peer)
    gg_copy = remote(gg_send, gg_in, pipe_peer)

    def out_grad(layer):
        for g in range(4):
            def body(k, carry):
                out = dot(v_t[layer, g], bm[layer, :, rows_of(g * 1024 + k * 512, 512)])

                @pl.when(pipe == layer)
                def _():
                    for h in range(4):
                        go_own[rows_of(g * 1024 + k * 512 + h * 128, 128), :] = (
                            out[:, h * 128:(h + 1) * 128]
                        )

                @pl.when(pipe != layer)
                def _():
                    for h in range(4):
                        go_send[rows_of(g * 1024 + k * 512 + h * 128, 128), :] = (
                            out[:, h * 128:(h + 1) * 128].astype(BF16)
                        )

                return carry

            lax.fori_loop(0, 2, body, 0)

    def small_grads(layer):
        def value_grad(k, total):
            cols = rows_of(k * 256, 256)
            return total + dot(nrm_t[layer, :, cols], vg[layer, cols, :])

        value_total = lax.fori_loop(0, 4, value_grad, jnp.zeros((128, 512), F32))

        def gain_grad(k, total):
            rows = rows_of(k * 128, 128)
            gained = ng[layer, rows, :] * xf[layer, rows, :].astype(F32) * rms_all[layer, rows, :]
            return total + jnp.sum(gained.reshape(16, 8, 128), axis=0)

        gain_total = lax.fori_loop(0, 8, gain_grad, jnp.zeros((8, 128), F32))

        @pl.when(pipe == layer)
        def _():
            gv_own[...] = value_total
            gg_own[...] = gain_total

        @pl.when(pipe != layer)
        def _():
            gv_send[...] = value_total.astype(BF16)
            gg_send[...] = gain_total
            gv_copy.start()
            gg_copy.start()

    def sum_up(copies, peers, at):
        for one in copies:
            one.wait()
        st[at + 1] = st[at] + st_in[at, 0] + st_in[at, 1] + st_in[at, 2]

    def main():
        yield from forward(1)
        mixture()
        yield
        out_project()
        copies = start([remote(st.at[0], st_in.at[0, k], peer) for k, peer in enumerate(t_peers)])
        yield
        turn_attention(1)
        targets()
        sum_up(copies, t_peers, 0)
        copies = start([remote(st.at[1], st_in.at[1, k], peer) for k, peer in enumerate(b_peers)])
        yield
        prepare(1)
        sum_up(copies, b_peers, 1)
        copies = start([remote(st.at[2], st_in.at[2, k], peer) for k, peer in enumerate(a_peers)])
        yield
        sum_up(copies, a_peers, 2)
        upstream(st[3])
        for layer in (1, 0):
            unmix(layer)
            turn = 2 + layer
            steps = scatter(layer, turn)
            next(steps)
            yield
            next(steps)
            out_grad(layer)
            yield
            yield from steps
            gr_all[layer, c, a, b] = scattered(turn).astype(BF16)
            steps = gather(gr_all.at[layer])
            next(steps)
            yield
            next(steps)
            if layer == 0:
                small_grads(1)
            yield
            yield from steps
            norm_back(layer)
            if layer == 1:
                input_grad(1)
        small_grads(0)
        yield

    def background():
        yield from forward(0)
        turn_attention(0)
        yield
        prepare(0)
        yield

    gains[pipe, 0:8, :] = jnp.broadcast_to(gain_ref[pl.ds(dp, 1), :], (8, 128))
    loads[0].wait()
    cross = [
        remote(gains.at[pipe], gains.at[pipe], pipe_peer),
        remote(wvb.at[pipe], wvb.at[pipe], pipe_peer),
    ]
    send_x(1)
    start(cross)
    att_cross.start()
    att_all[pipe, c, a, b, xh] = att_ref[pipe]
    for m in range(4):
        rows = x_ref[m * 32:(m + 1) * 32, :].astype(F32)
        sq[m] = jnp.broadcast_to(jnp.sum(rows * rows, axis=1, keepdims=True), (32, 128))
    sq_in[pipe, tensor] = sq[pipe * 2 + c]
    squares = []
    for peer in t_peers:
        own = lax.rem(peer["tensor"], 2)
        squares.append(remote(sq.at[pipe * 2 + own], sq_in.at[pipe, tensor], peer))
        squares.append(remote(
            sq.at[other * 2 + own], sq_in.at[pipe, tensor], {"tensor": peer["tensor"], "pipe": other}
        ))
    squares.append(remote(sq.at[other * 2 + c], sq_in.at[pipe, tensor], pipe_peer))
    start(squares)
    attention1 = gather_attention(1)
    next(attention1)
    loads[1].wait()

    def turn_w(layer):
        def body(k, carry):
            wq[layer, rows_of(k * 128, 128), :] = wb[layer, rows_of(k * 128, 128), :].T
            return carry

        lax.fori_loop(0, 32, body, 0)
        for k in range(4):
            wvt[layer, k * 128:(k + 1) * 128, :] = wvb[layer, :, k * 128:(k + 1) * 128].T

    v_bd[...] = jnp.zeros_like(v_bd)
    up_bd[...] = jnp.zeros_like(up_bd)
    finish(squares)
    for layer in range(2):
        squared = sq_in[layer, 0] + sq_in[layer, 1] + sq_in[layer, 2] + sq_in[layer, 3]
        rms_own[layer] = lax.rsqrt(squared / D + EPS)
    finish(cross)
    next(attention1)

    @pl.when(pipe == 1)
    def _():
        att_cross.wait_send()

    w_copies = [
        remote(wb.at[pipe, k * 512:(k + 1) * 512], wb.at[pipe, k * 512:(k + 1) * 512], pipe_peer)
        for k in range(8)
    ]

    def pieces(copies, sender):
        for one in copies:
            @pl.when(pipe == sender)
            def _():
                one.start()

            yield

    def weights(layer):
        for _ in pieces(w_copies, layer):
            yield
        for one in w_copies:
            @pl.when(pipe == layer)
            def _():
                one.wait_send()

            @pl.when(pipe != layer)
            def _():
                one.wait_recv()

        yield
        turn_w(layer)
        yield

    def send_other_x():
        send_x(0)
        yield

    streams = {
        "m": main(), "g": background(), "a": attention1, "b": gather_attention(0),
        "w": weights(1), "u": weights(0), "s": send_other_x(),
        "o": pieces(go_copies, 0), "q": pieces(go_copies, 1),
    }
    for name in ORDER:
        next(streams[name])

    @pl.when(pipe == 0)
    def _():
        att_cross.wait_send()

    def add_halves(k, carry):
        rows = rows_of(k * 256, 256)
        go_ref[rows, :] = (go_own[rows, :] + go_in[rows, :].astype(F32)).astype(BF16)
        return carry

    for one in go_copies:
        one.wait()
    lax.fori_loop(0, 16, add_halves, 0)
    gv_copy.wait()
    gg_copy.wait()
    gv_ref[...] = (gv_own[...] + gv_in[...].astype(F32)).astype(BF16)
    gg_ref[...] = jnp.sum(gg_own[...] + gg_in[...], axis=0, keepdims=True)


def shards(
    layer_inputs, norm_gain, value_weight, out_weight, scores, head_weight, lengths, returns,
    response_mask,
):
    replica = lax.axis_index("dp")
    own_lengths = lax.dynamic_index_in_dim(lengths, replica, 0, keepdims=False)
    attention = attention_weights(scores[0, 0], own_lengths)
    packed = attention.reshape(2, 2, 2, 4, 32, 32).transpose(0, 3, 4, 2, 1, 5).reshape(2, 128, 128)
    position = jnp.arange(128, dtype=jnp.int32)
    block_len = jnp.repeat(own_lengths, 32, total_repeat_length=128)
    live = ((position % 32 < block_len) & (response_mask == 1)).astype(F32)
    high = returns.astype(BF16)
    rest = returns - high.astype(F32)
    middle = rest.astype(BF16)
    low = (rest - middle.astype(F32)).astype(BF16)
    extra = jnp.stack([high, middle, low, live.astype(BF16)])
    extra = jnp.concatenate([extra, jnp.zeros((12, 128), BF16)], axis=0)
    packet = jnp.concatenate([packed, jnp.broadcast_to(extra, (2, 16, 128))], axis=1)

    vmem = pl.BlockSpec(memory_space=pltpu.VMEM)
    anywhere = pl.BlockSpec(memory_space=pl.ANY)

    def scratch(*shape, dtype=BF16):
        return pltpu.VMEM(shape, dtype)

    grad_out, grad_value, grad_gain = pl.pallas_call(
        kernel,
        out_shape=(
            jax.ShapeDtypeStruct((4096, 128), BF16),
            jax.ShapeDtypeStruct((128, 512), BF16),
            jax.ShapeDtypeStruct((1, 128), F32),
        ),
        in_specs=[vmem, vmem, vmem, anywhere, anywhere, vmem],
        out_specs=(vmem, vmem, vmem),
        scratch_shapes=[
            scratch(2, 2, 4, 4, 2, 144, 128),
            scratch(2, 2, 4, 4, 32, 640),
            scratch(2, 1024, 128),
            scratch(4, 2, 4, 4, 32, 512),
            scratch(4, 4, 32, 512),
            scratch(4, 4, 4, 32, 512),
            scratch(4, 3, 4, 32, 512),
            scratch(4, 3, 32, 512),
            scratch(4, 4, 32, 512),
            scratch(2, 2, 4, 4, 32, 512),
            scratch(4, 32, 128, dtype=F32),
            scratch(2, 4, 32, 128, dtype=F32),
            scratch(2, 1024, 4096),
            scratch(2, 16, 2, 256, 128),
            scratch(4, 4, 128, 512),
            scratch(2, 128, 512),
            scratch(2, 4096, 128),
            scratch(2, 4096, 128),
            scratch(2, 128, 512),
            scratch(2, 512, 128),
            scratch(2, 8, 128, dtype=F32),
            scratch(2, 32, 128, dtype=F32),
            scratch(2, 1024, 128, dtype=F32),
            scratch(1024, 128, dtype=F32),
            scratch(4, 16, 128, dtype=F32),
            scratch(3, 3, 16, 128, dtype=F32),
            scratch(128, 128, dtype=F32),
            scratch(32, 128, dtype=F32),
            scratch(2, 2, 8, 128, dtype=F32),
            scratch(2, 1024, 128),
            scratch(2, 1024, 128, dtype=F32),
            scratch(2, 1024, 512),
            scratch(2, 4, 128, 1024),
            scratch(2, 128, 1024),
            scratch(4096, 128, dtype=F32),
            scratch(4096, 128),
            scratch(4096, 128),
            scratch(128, 512, dtype=F32),
            scratch(128, 512),
            scratch(128, 512),
            scratch(8, 128, dtype=F32),
            scratch(8, 128, dtype=F32),
            scratch(8, 128, dtype=F32),
            pltpu.SemaphoreType.DMA((COPIES,)),
            pltpu.SemaphoreType.DMA((COPIES,)),
            pltpu.SemaphoreType.DMA((2,)),
        ],
        compiler_params=pltpu.CompilerParams(
            collective_id=0, has_side_effects=True, vmem_limit_bytes=60 * 1024 * 1024
        ),
        cost_estimate=pl.CostEstimate(
            flops=8_000_000_000, bytes_accessed=6_000_000, transcendentals=0
        ),
    )(
        packet,
        layer_inputs[0],
        norm_gain[0].reshape(16, 128),
        value_weight[0],
        out_weight[0],
        head_weight.astype(F32).reshape(16, 128),
    )
    return grad_out[None], grad_value[None], grad_gain


def solution(mesh):
    return jax.shard_map(
        shards,
        mesh=mesh,
        in_specs=(
            P("pipe", "dp", "tensor"),
            P("pipe", "tensor"),
            P("pipe", ("tensor", "dp"), None),
            P("pipe", None, ("tensor", "dp")),
            P("pipe", "dp", None, "tensor", None, None),
            P("tensor"),
            P(),
            P("dp"),
            P("dp"),
        ),
        out_specs=(
            P("pipe", None, ("tensor", "dp")),
            P("pipe", ("tensor", "dp"), None),
            P("pipe", ("tensor", "dp")),
        ),
        check_vma=False,
    )
```

```python
import jax
import jax.numpy as jnp
from jax import lax
from jax.experimental import pallas as pl
from jax.experimental.pallas import tpu as pltpu
from jax.sharding import PartitionSpec as P

D = 8192
HD = 128
KVH = 4
EPS = 1e-05
F32 = jnp.float32
BF16 = jnp.bfloat16
MESH = pl.DeviceIdType.MESH
COPIES = 200
ORDER = (
    "mw",
    "maww",
    "m",
    "maw",
    "mww",
    "maws",
    "mww",
    "mw",
    "mbuu",
    "muug",
    "muubug",
    "mug",
    "mbg",
    "mubg",
    "moog",
    "mboug",
    "mgoo",
    "mooqqq",
    "m",
    "moq",
    "mqq",
    "mqq",
    "m",
)


def dot(left, right):
    return jnp.dot(left, right, preferred_element_type=F32)


def split_pair(value):
    high = value.astype(BF16)
    return high, (value - high.astype(F32)).astype(BF16)


def kernel(
    score_ref, length_ref, return_ref, mask_ref, x_ref, gain_ref, wv_ref, w_ref, head_ref,
    go_own, go_in, gv_ref, gg_ref,
    att_own, att_all, v_all, xf, part, sum1, r0, r1, r2, r2x, gr_all,
    sq, sq_in, bm, att_t, v_bd, up_bd, wb, wq, wvb, wvt, gains, rms_own, rms_all, hid, st, st_in,
    coef, ret, err_at, up, ng, vg, v_t, nrm_t, go_keep, go_send, gv_own, gv_send, gv_in,
    gg_own, gg_send, gg_in,
    send_sems, recv_sems, local_sems,
):
    pipe = lax.axis_index("pipe")
    tensor = lax.axis_index("tensor")
    dp = lax.axis_index("dp")
    c = lax.rem(tensor, 2)
    xh = lax.div(tensor, 2)
    z = lax.div(dp, 4)
    y = lax.rem(dp, 4)
    a = jnp.where(c == 0, z, y)
    b = jnp.where(c == 0, y, z)
    other = 1 - pipe

    def dp_of(a_at, b_at):
        return jnp.where(c == 0, a_at * 4 + b_at, b_at * 4 + a_at)

    core_peer = {"tensor": xh * 2 + 1 - c}
    x_tensor = (1 - xh) * 2 + c
    x_peer = {"tensor": x_tensor}
    pipe_peer = {"pipe": other}
    a_next = [lax.rem(a + k, 4) for k in (1, 2, 3)]
    b_next = [lax.rem(b + k, 4) for k in (1, 2, 3)]
    a_peers = [{"dp": dp_of(at, b)} for at in a_next]
    ax_peers = [{"dp": dp_of(at, b), "tensor": x_tensor} for at in [a] + a_next]
    b_peers = [{"dp": dp_of(a, bt)} for bt in b_next]
    t_peers = [{"tensor": lax.rem(tensor + k, 4)} for k in (1, 2, 3)]
    dp_next = [lax.rem(dp + k, 16) for k in range(16)]
    used = [0]

    def remote(src, dst, device):
        at = used[0]
        used[0] += 1
        return pltpu.make_async_remote_copy(
            src_ref=src, dst_ref=dst, send_sem=send_sems.at[at], recv_sem=recv_sems.at[at],
            device_id=device, device_id_type=MESH,
        )

    def start(copies):
        for one in copies:
            one.start()
        return copies

    def finish(copies):
        for one in copies:
            one.wait()

    def rows_of(first, size):
        return pl.ds(pl.multiple_of(first, size), size)

    loads = [
        pltpu.make_async_copy(wv_ref, wvb.at[pipe], local_sems.at[0]),
        pltpu.make_async_copy(w_ref, wb.at[pipe], local_sems.at[1]),
    ]
    start(loads)
    barrier = pltpu.get_barrier_semaphore()
    partners = [{"dp": to} for to in dp_next[1:]] + t_peers + ax_peers[1:]
    partners += [{"dp": to, "pipe": other} for to in dp_next]
    partners += [{"tensor": one["tensor"], "pipe": other} for one in t_peers]
    for peer in partners:
        pl.semaphore_signal(barrier, inc=1, device_id=peer, device_id_type=MESH)
    pl.semaphore_wait(barrier, len(partners))

    def x_copy(to, device, half):
        return remote(
            x_ref.at[rows_of(half * 64, 64), rows_of(to * 128, 128)],
            xf.at[pipe, rows_of(dp * 64, 64)], device,
        )

    x_same = [x_copy(to, {"dp": to}, pipe) for to in dp_next[1:]]
    x_cross = [x_copy(to, {"dp": to, "pipe": other}, other) for to in dp_next]

    def send_x(layer):
        @pl.when(pipe == layer)
        def _():
            start(x_cross)
            start(x_same)
            xf[layer, rows_of(dp * 64, 64), :] = x_ref[rows_of(layer * 64, 64), rows_of(dp * 128, 128)]

    def wait_x(layer):
        @pl.when(pipe == layer)
        def _():
            finish(x_same)
            for one in x_cross:
                one.wait_send()

        @pl.when(pipe != layer)
        def _():
            for one in x_cross:
                one.wait_recv()

    att_cross = remote(att_own.at[other], att_all.at[pipe, c, a, b, xh], pipe_peer)

    def attend():
        row = lax.rem(lax.broadcasted_iota(jnp.int32, (256, 32), 0), 32)
        key = lax.broadcasted_iota(jnp.int32, (256, 32), 1)
        span = [length_ref[m, dp] for m in range(4)]
        weights = []
        for m in range(4):
            allowed = (key <= row) & (key < span[m])
            masked = jnp.where(allowed, score_ref[m].astype(F32).reshape(256, 32), -1e30)
            top = jnp.max(masked, axis=1, keepdims=True)
            exponent = jnp.where(allowed, jnp.exp(masked - top), 0.0)
            weights.append(exponent / jnp.sum(exponent, axis=1, keepdims=True))
        position = lax.broadcasted_iota(jnp.int32, (1, 128), 1)
        block = lax.div(position, 32)
        length = jnp.where(block == 0, span[0], span[1])
        length = jnp.where(block == 2, span[2], length)
        length = jnp.where(block == 3, span[3], length)
        live = ((lax.rem(position, 32) < length) & (mask_ref[...] == 1)).astype(F32)
        returns = return_ref[...]
        high = returns.astype(BF16).astype(F32)
        middle = (returns - high).astype(BF16).astype(F32)
        low = (returns - high - middle).astype(BF16).astype(F32)
        at = lax.broadcasted_iota(jnp.int32, (16, 128), 0)
        extra = jnp.where(at == 0, high, jnp.where(at == 1, middle, jnp.where(at == 2, low, 0.0)))
        extra = jnp.where(at == 3, live, extra).astype(BF16)
        for half in range(2):
            tile = [
                weights[half * 2 + m][q * 128:(q + 1) * 128] for q in range(2) for m in range(2)
            ]
            att_own[half, 0:128, :] = jnp.concatenate(tile, axis=1).astype(BF16)
            att_own[half, 128:144, :] = extra

    def gather_attention(layer):
        here = att_all.at[layer]

        @pl.when(pipe != layer)
        def _():
            att_cross.wait_recv()

        copies = start([remote(here.at[c, a, b, xh], here.at[c, a, b, xh], x_peer)])
        yield
        finish(copies)
        copies = start([remote(here.at[c, a, b], here.at[c, a, b], peer) for peer in a_peers])
        yield
        finish(copies)
        copies = start([remote(here.at[c, :, b], here.at[c, :, b], peer) for peer in b_peers])
        yield
        finish(copies)
        copies = start([remote(here.at[c], here.at[c], core_peer)])
        yield
        finish(copies)
        yield

    def scatter(layer, turn):
        here = part.at[layer]
        copies = start([remote(here.at[1 - c], r0.at[turn], core_peer)])
        yield
        finish(copies)

        def add0(at, carry):
            for bt in range(4):
                part[layer, c, at, bt] = (
                    part[layer, c, at, bt].astype(F32) + r0[turn, at, bt].astype(F32)
                ).astype(BF16)
            return carry

        lax.fori_loop(0, 4, add0, 0)
        copies = start([
            remote(here.at[c, :, bt], r1.at[turn, k], peer)
            for k, (bt, peer) in enumerate(zip(b_next, b_peers))
        ])
        yield
        finish(copies)
        for at in range(4):
            sum1[turn, at] = (
                part[layer, c, at, b].astype(F32) + r1[turn, 0, at].astype(F32)
                + r1[turn, 1, at].astype(F32) + r1[turn, 2, at].astype(F32)
            ).astype(BF16)
        copies = [
            remote(sum1.at[turn, at], r2x.at[turn, k], peer)
            for k, (at, peer) in enumerate(zip([a] + a_next, ax_peers))
        ]
        copies += [
            remote(sum1.at[turn, at], r2.at[turn, k], peer)
            for k, (at, peer) in enumerate(zip(a_next, a_peers))
        ]
        start(copies)
        yield
        finish(copies)

    def scattered(turn):
        total = sum1[turn, a].astype(F32)
        for k in range(3):
            total = total + r2[turn, k].astype(F32)
        for k in range(4):
            total = total + r2x[turn, k].astype(F32)
        return total

    def gather(here):
        copies = start([remote(here.at[c, a, b], here.at[c, a, b], peer) for peer in a_peers])
        yield
        finish(copies)
        copies = start([remote(here.at[c, :, b], here.at[c, :, b], peer) for peer in b_peers])
        yield
        finish(copies)
        copies = start([remote(here.at[c], here.at[c], core_peer)])
        yield
        finish(copies)

    heads = head_ref[...].astype(F32)
    head_at = lax.broadcasted_iota(jnp.int32, (16, 128), 0)
    head_row = jnp.sum(jnp.where(head_at == dp, heads, 0.0), axis=0, keepdims=True)
    lane = lax.broadcasted_iota(jnp.int32, (128, 128), 1)

    def project(layer):
        gain_row = gains[layer, 0:1, :]

        def body(zi, carry):
            xg = (xf[layer, rows_of(zi * 256, 256), :].astype(F32) * gain_row).astype(BF16)
            out = dot(xg, wvb[layer]).astype(BF16)
            for yi in range(4):
                part[layer, 0, zi, yi] = out[yi * 64:yi * 64 + 32]
                part[layer, 1, yi, zi] = out[yi * 64 + 32:yi * 64 + 64]
            return carry

        lax.fori_loop(0, 4, body, 0)

    def forward(layer):
        wait_x(layer)
        project(layer)
        yield from scatter(layer, layer)
        rms = rms_own[layer, :, 0:1]
        total = scattered(layer) * rms
        high, low = split_pair(rms)
        place = lax.broadcasted_iota(jnp.int32, (32, 128), 1)
        extra = jnp.where(place == 0, high.astype(F32), jnp.where(place == 1, low.astype(F32), 0.0))
        v_all[layer, c, a, b, :, 0:512] = total.astype(BF16)
        v_all[layer, c, a, b, :, 512:640] = extra.astype(BF16)
        yield from gather(v_all.at[layer])

    def mixture():
        def body(zi, carry):
            for yi in range(4):
                first = pl.multiple_of(zi * 256 + yi * 64, 64)
                for g in range(4):
                    places = (0, zi, yi) if g % 2 == 0 else (1, yi, zi)
                    att = att_all[(1, *places, g // 2)][0:128, :]
                    cols = slice(g * 128, (g + 1) * 128)
                    for m in range(2):
                        values = v_all[(1, 0, zi, yi) if m == 0 else (1, 1, yi, zi)][:, cols]
                        for q in range(2):
                            at = q * 2 + m
                            v_bd[yi, g, at * 32:(at + 1) * 32, at * 128:(at + 1) * 128] = values
                    out = dot(att, v_bd[yi, g]).astype(BF16)
                    for h in range(4):
                        for q in range(2):
                            for m in range(2):
                                head = g * 8 + q * 4 + h
                                bm[1, pl.ds(first + m * 32, 32), head * 128:(head + 1) * 128] = (
                                    out[h * 32:(h + 1) * 32, (q * 2 + m) * 128:(q * 2 + m + 1) * 128]
                                )
            return carry

        lax.fori_loop(0, 4, body, 0)

    def out_project():
        def body(k, carry):
            rows = rows_of(k * 512, 512)
            hid[rows, :] = xf[1, rows, :].astype(F32) + dot(bm[1, rows, :], wb[1])
            return carry

        lax.fori_loop(0, 2, body, 0)
        tile = jnp.zeros((128, 128), F32)
        for k in range(8):
            h = hid[k * 128:(k + 1) * 128, :]
            tile = jnp.where(lane == k, jnp.sum(h * h, axis=1, keepdims=True), tile)
            tile = jnp.where(lane == 8 + k, jnp.sum(h * head_row, axis=1, keepdims=True), tile)
        st[0] = tile.T[0:16]

    def targets():
        for d in range(16):
            extra = att_all[1, 0, d // 4, d % 4, 0, 128:144, :].astype(F32)
            at = 8 * (d % 2) + d // 2
            ret[at:at + 1, :] = extra[0:1] + extra[1:2] + extra[2:3]
            ret[16 + at:17 + at, :] = extra[3:4]
        returns = ret[0:16, :]
        live = ret[16:32, :]

        def whole(value):
            return jnp.sum(jnp.sum(value, axis=1, keepdims=True), axis=0, keepdims=True)

        count = jnp.maximum(whole(live), 1.0)
        mean = whole(live * returns) / count
        spread = whole(live * (returns - mean) * (returns - mean)) / count
        target = (returns - mean) * lax.rsqrt(spread + EPS)
        low = lax.broadcasted_iota(jnp.int32, (8, 128), 1) < 64
        for at, value in enumerate((target, live)):
            even, odd = value[0:8], value[8:16]
            err_at[0, at] = jnp.where(low, even, pltpu.roll(odd, 64, 1))
            err_at[1, at] = jnp.where(low, pltpu.roll(even, 64, 1), odd)

    def upstream(sums):
        target, live = err_at[pipe, 0], err_at[pipe, 1]
        out_scale = lax.rsqrt(sums[0:8] / D + EPS)
        critic = out_scale * sums[8:16]
        alpha = live * (critic - target) * out_scale
        beta = alpha * out_scale * critic / D
        coef[...] = jnp.concatenate([alpha, beta, jnp.zeros((112, 128), F32)], axis=0).T
        for k in range(8):
            rows = slice(k * 128, (k + 1) * 128)
            up[1, rows, :] = (
                coef[:, k:k + 1] * head_row - coef[:, 8 + k:9 + k] * hid[rows, :]
            ).astype(BF16)

    def turn_attention(layer):
        def body(zi, carry):
            for yi in range(4):
                for g in range(4):
                    places = (0, zi, yi) if g % 2 == 0 else (1, yi, zi)
                    turned = att_all[(layer, *places, g // 2)][0:128, :].T
                    for q in range(2):
                        for m in range(2):
                            att_t[layer, zi * 4 + yi, m, (g * 2 + q) * 32:(g * 2 + q + 1) * 32, :] = (
                                turned[(q * 2 + m) * 32:(q * 2 + m + 1) * 32]
                            )
            return carry

        lax.fori_loop(0, 4, body, 0)

    def prepare(layer):
        gain_row = gains[layer, 0:1, :]

        def body(zi, carry):
            for pair in range(2):
                first = pl.multiple_of(zi * 256 + pair * 128, 128)
                packets = []
                for yi in (pair * 2, pair * 2 + 1):
                    packets.append(v_all.at[layer, 0, zi, yi])
                    packets.append(v_all.at[layer, 1, yi, zi])
                extra = jnp.concatenate([one[:, 512:640] for one in packets], axis=0).astype(F32)
                rms = extra[:, 0:1] + extra[:, 1:2]
                rms_all[layer, pl.ds(first, 128), :] = jnp.broadcast_to(rms, (128, 128))
                normed = xf[layer, pl.ds(first, 128), :].astype(F32) * rms * gain_row
                nrm_t[layer, :, pl.ds(first, 128)] = normed.astype(BF16).T
                for g in range(4):
                    cols = slice(g * 128, (g + 1) * 128)
                    values = jnp.concatenate([one[:, cols] for one in packets], axis=0)
                    v_t[layer, g, :, pl.ds(first, 128)] = values.T
            return carry

        lax.fori_loop(0, 4, body, 0)

    def unmix(layer):
        def spread(d, carry):
            for m in range(2):
                first = pl.multiple_of(d * 64 + m * 32, 32)
                rows = up[layer, pl.ds(first, 32), :]
                for h in range(4):
                    up_bd[m, h * 32:(h + 1) * 32, h * 128:(h + 1) * 128] = rows
                out = dot(att_t[layer, d, m], up_bd[m]).astype(BF16)
                for q in range(8):
                    bm[layer, pl.ds(first, 32), q * 512:(q + 1) * 512] = out[q * 32:(q + 1) * 32, :]
            return carry

        lax.fori_loop(0, 16, spread, 0)

        def body(k, carry):
            rows = rows_of(k * 512, 512)
            for g in range(4):
                cols = slice(g * 1024, (g + 1) * 1024)
                out = dot(bm[layer, rows, cols], wq[layer, cols, :]).astype(BF16)
                for zi in range(2):
                    for yi in range(4):
                        first = zi * 256 + yi * 64
                        into = slice(g * 128, (g + 1) * 128)
                        part[layer, 0, k * 2 + zi, yi, :, into] = out[first:first + 32]
                        part[layer, 1, yi, k * 2 + zi, :, into] = out[first + 32:first + 64]
            return carry

        lax.fori_loop(0, 2, body, 0)

    def norm_back(layer):
        def body(zi, carry):
            first = pl.multiple_of(zi * 256, 256)
            for yi in range(4):
                vg[layer, pl.ds(first + yi * 64, 32), :] = gr_all[layer, 0, zi, yi]
                vg[layer, pl.ds(first + yi * 64 + 32, 32), :] = gr_all[layer, 1, yi, zi]
            ng[layer, pl.ds(first, 256), :] = dot(vg[layer, pl.ds(first, 256), :], wvt[layer])
            return carry

        lax.fori_loop(0, 4, body, 0)

    def input_grad(layer):
        gain_row = gains[layer, 0:1, :]

        def body(zi, carry):
            for yi in range(4):
                for m in range(2):
                    rows = pl.ds(pl.multiple_of(zi * 256 + yi * 64 + m * 32, 32), 32)
                    values = v_all[(layer, 0, zi, yi) if m == 0 else (layer, 1, yi, zi)][:, 0:512]
                    product = vg[layer, rows, :].astype(F32) * values.astype(F32)
                    inner = jnp.sum(product, axis=1, keepdims=True)
                    rms = rms_all[layer, rows, :]
                    up[layer - 1, rows, :] = (
                        up[layer, rows, :].astype(F32) + rms * gain_row * ng[layer, rows, :]
                        - (rms * rms * (inner / D)) * xf[layer, rows, :].astype(F32)
                    ).astype(BF16)
            return carry

        lax.fori_loop(0, 4, body, 0)

    go_copies = [
        remote(go_send.at[k * 512:(k + 1) * 512], go_in.at[k * 512:(k + 1) * 512], pipe_peer)
        for k in range(8)
    ]
    keep = pltpu.make_async_copy(go_keep, go_own, local_sems.at[2])
    gv_copy = remote(gv_send, gv_in, pipe_peer)
    gg_copy = remote(gg_send, gg_in, pipe_peer)

    def out_grad(layer):
        for g in range(4):
            def body(k, carry):
                out = dot(v_t[layer, g], bm[layer, :, rows_of(g * 1024 + k * 512, 512)])

                @pl.when(pipe == layer)
                def _():
                    for h in range(4):
                        go_keep[rows_of(g * 1024 + k * 512 + h * 128, 128), :] = (
                            out[:, h * 128:(h + 1) * 128].astype(BF16)
                        )

                @pl.when(pipe != layer)
                def _():
                    for h in range(4):
                        go_send[rows_of(g * 1024 + k * 512 + h * 128, 128), :] = (
                            out[:, h * 128:(h + 1) * 128].astype(BF16)
                        )

                return carry

            lax.fori_loop(0, 2, body, 0)

        @pl.when(pipe == layer)
        def _():
            keep.start()

    def small_grads(layer):
        def value_grad(k, total):
            cols = rows_of(k * 256, 256)
            return total + dot(nrm_t[layer, :, cols], vg[layer, cols, :])

        value_total = lax.fori_loop(0, 4, value_grad, jnp.zeros((128, 512), F32))

        def gain_grad(k, total):
            rows = rows_of(k * 128, 128)
            gained = ng[layer, rows, :] * xf[layer, rows, :].astype(F32) * rms_all[layer, rows, :]
            return total + jnp.sum(gained.reshape(16, 8, 128), axis=0)

        gain_total = lax.fori_loop(0, 8, gain_grad, jnp.zeros((8, 128), F32))

        @pl.when(pipe == layer)
        def _():
            gv_own[...] = value_total
            gg_own[...] = gain_total

        @pl.when(pipe != layer)
        def _():
            gv_send[...] = value_total.astype(BF16)
            gg_send[...] = gain_total
            gv_copy.start()
            gg_copy.start()

    def sum_up(copies, peers, at):
        for one in copies:
            one.wait()
        st[at + 1] = st[at] + st_in[at, 0] + st_in[at, 1] + st_in[at, 2]

    def main():
        yield from forward(1)
        mixture()
        yield
        out_project()
        copies = start([remote(st.at[0], st_in.at[0, k], peer) for k, peer in enumerate(t_peers)])
        yield
        turn_attention(1)
        targets()
        sum_up(copies, t_peers, 0)
        copies = start([remote(st.at[1], st_in.at[1, k], peer) for k, peer in enumerate(b_peers)])
        yield
        prepare(1)
        sum_up(copies, b_peers, 1)
        copies = start([remote(st.at[2], st_in.at[2, k], peer) for k, peer in enumerate(a_peers)])
        yield
        sum_up(copies, a_peers, 2)
        upstream(st[3])
        for layer in (1, 0):
            unmix(layer)
            turn = 2 + layer
            steps = scatter(layer, turn)
            next(steps)
            yield
            next(steps)
            out_grad(layer)
            yield
            yield from steps
            gr_all[layer, c, a, b] = scattered(turn).astype(BF16)
            steps = gather(gr_all.at[layer])
            next(steps)
            yield
            next(steps)
            if layer == 0:
                small_grads(1)
            yield
            yield from steps
            norm_back(layer)
            if layer == 1:
                input_grad(1)
        small_grads(0)
        yield

    def background():
        yield from forward(0)
        turn_attention(0)
        yield
        prepare(0)
        yield

    gains[pipe, 0:8, :] = jnp.broadcast_to(gain_ref[:, rows_of(dp * 128, 128)], (8, 128))
    loads[0].wait()
    cross = [
        remote(gains.at[pipe], gains.at[pipe], pipe_peer),
        remote(wvb.at[pipe], wvb.at[pipe], pipe_peer),
    ]
    send_x(1)
    start(cross)
    attend()
    att_cross.start()
    att_all[pipe, c, a, b, xh] = att_own[pipe]
    for m in range(4):
        rows = x_ref[m * 32:(m + 1) * 32, :].astype(F32)
        sq[m] = jnp.broadcast_to(jnp.sum(rows * rows, axis=1, keepdims=True), (32, 128))
    sq_in[pipe, tensor] = sq[pipe * 2 + c]
    squares = []
    for peer in t_peers:
        own = lax.rem(peer["tensor"], 2)
        squares.append(remote(sq.at[pipe * 2 + own], sq_in.at[pipe, tensor], peer))
        squares.append(remote(
            sq.at[other * 2 + own], sq_in.at[pipe, tensor], {"tensor": peer["tensor"], "pipe": other}
        ))
    squares.append(remote(sq.at[other * 2 + c], sq_in.at[pipe, tensor], pipe_peer))
    start(squares)
    attention1 = gather_attention(1)
    next(attention1)
    loads[1].wait()

    def turn_w(layer):
        def body(k, carry):
            wq[layer, rows_of(k * 128, 128), :] = wb[layer, rows_of(k * 128, 128), :].T
            return carry

        lax.fori_loop(0, 32, body, 0)
        for k in range(4):
            wvt[layer, k * 128:(k + 1) * 128, :] = wvb[layer, :, k * 128:(k + 1) * 128].T

    v_bd[...] = jnp.zeros_like(v_bd)
    up_bd[...] = jnp.zeros_like(up_bd)
    finish(squares)
    for layer in range(2):
        squared = sq_in[layer, 0] + sq_in[layer, 1] + sq_in[layer, 2] + sq_in[layer, 3]
        rms_own[layer] = lax.rsqrt(squared / D + EPS)
    finish(cross)
    next(attention1)

    @pl.when(pipe == 1)
    def _():
        att_cross.wait_send()

    w_copies = [
        remote(wb.at[pipe, k * 512:(k + 1) * 512], wb.at[pipe, k * 512:(k + 1) * 512], pipe_peer)
        for k in range(8)
    ]

    def pieces(copies, sender):
        for one in copies:
            @pl.when(pipe == sender)
            def _():
                one.start()

            yield

    def weights(layer):
        for _ in pieces(w_copies, layer):
            yield
        for one in w_copies:
            @pl.when(pipe == layer)
            def _():
                one.wait_send()

            @pl.when(pipe != layer)
            def _():
                one.wait_recv()

        yield
        turn_w(layer)
        yield

    def send_other_x():
        send_x(0)
        yield

    streams = {
        "m": main(), "g": background(), "a": attention1, "b": gather_attention(0),
        "w": weights(1), "u": weights(0), "s": send_other_x(),
        "o": pieces(go_copies, 0), "q": pieces(go_copies, 1),
    }
    for names in ORDER:
        for name in names:
            next(streams[name])

    @pl.when(pipe == 0)
    def _():
        att_cross.wait_send()

    for one in go_copies:
        one.wait()
    keep.wait()
    gv_copy.wait()
    gg_copy.wait()
    gv_ref[...] = (gv_own[...] + gv_in[...].astype(F32)).astype(BF16)
    gg_ref[...] = jnp.sum(gg_own[...] + gg_in[...], axis=0, keepdims=True)


def add_halves(own_ref, other_ref, value_ref, gain_ref, go_ref, gv_ref, gg_ref):
    go_ref[...] = (own_ref[...].astype(F32) + other_ref[...].astype(F32)).astype(BF16)

    @pl.when(pl.program_id(0) == 0)
    def _():
        gv_ref[...] = value_ref[...]
        gg_ref[...] = gain_ref[...]


def shards(
    layer_inputs, norm_gain, value_weight, out_weight, scores, head_weight, lengths, returns,
    response_mask,
):
    vmem = pl.BlockSpec(memory_space=pltpu.VMEM)
    anywhere = pl.BlockSpec(memory_space=pl.ANY)
    smem = pl.BlockSpec(memory_space=pltpu.SMEM)

    def scratch(*shape, dtype=BF16):
        return pltpu.VMEM(shape, dtype)

    own_out, other_out, grad_value, grad_gain = pl.pallas_call(
        kernel,
        out_shape=(
            jax.ShapeDtypeStruct((4096, 128), BF16),
            jax.ShapeDtypeStruct((4096, 128), BF16),
            jax.ShapeDtypeStruct((128, 512), BF16),
            jax.ShapeDtypeStruct((1, 128), F32),
        ),
        in_specs=[vmem, smem, vmem, vmem, vmem, vmem, anywhere, anywhere, vmem],
        out_specs=(anywhere, anywhere, vmem, vmem),
        scratch_shapes=[
            scratch(2, 144, 128),
            scratch(2, 2, 4, 4, 2, 144, 128),
            scratch(2, 2, 4, 4, 32, 640),
            scratch(2, 1024, 128),
            scratch(2, 2, 4, 4, 32, 512),
            scratch(4, 4, 32, 512),
            scratch(4, 4, 4, 32, 512),
            scratch(4, 3, 4, 32, 512),
            scratch(4, 3, 32, 512),
            scratch(4, 4, 32, 512),
            scratch(2, 2, 4, 4, 32, 512),
            scratch(4, 32, 128, dtype=F32),
            scratch(2, 4, 32, 128, dtype=F32),
            scratch(2, 1024, 4096),
            scratch(2, 16, 2, 256, 128),
            scratch(4, 4, 128, 512),
            scratch(2, 128, 512),
            scratch(2, 4096, 128),
            scratch(2, 4096, 128),
            scratch(2, 128, 512),
            scratch(2, 512, 128),
            scratch(2, 8, 128, dtype=F32),
            scratch(2, 32, 128, dtype=F32),
            scratch(2, 1024, 128, dtype=F32),
            scratch(1024, 128, dtype=F32),
            scratch(4, 16, 128, dtype=F32),
            scratch(3, 3, 16, 128, dtype=F32),
            scratch(128, 128, dtype=F32),
            scratch(32, 128, dtype=F32),
            scratch(2, 2, 8, 128, dtype=F32),
            scratch(2, 1024, 128),
            scratch(2, 1024, 128, dtype=F32),
            scratch(2, 1024, 512),
            scratch(2, 4, 128, 1024),
            scratch(2, 128, 1024),
            scratch(4096, 128),
            scratch(4096, 128),
            scratch(128, 512, dtype=F32),
            scratch(128, 512),
            scratch(128, 512),
            scratch(8, 128, dtype=F32),
            scratch(8, 128, dtype=F32),
            scratch(8, 128, dtype=F32),
            pltpu.SemaphoreType.DMA((COPIES,)),
            pltpu.SemaphoreType.DMA((COPIES,)),
            pltpu.SemaphoreType.DMA((3,)),
        ],
        compiler_params=pltpu.CompilerParams(
            collective_id=0, has_side_effects=True, vmem_limit_bytes=60 * 1024 * 1024
        ),
        cost_estimate=pl.CostEstimate(
            flops=8_000_000_000, bytes_accessed=6_000_000, transcendentals=0
        ),
    )(
        scores[0, 0],
        lengths.T,
        returns.reshape(1, 128),
        response_mask.reshape(1, 128),
        layer_inputs[0],
        norm_gain,
        value_weight[0],
        out_weight[0],
        head_weight.reshape(16, 128),
    )
    quarter = pl.BlockSpec((1024, 128), lambda k: (k, 0))
    value_block = pl.BlockSpec((128, 512), lambda k: (0, 0))
    gain_block = pl.BlockSpec((1, 128), lambda k: (0, 0))
    grad_out, grad_value, grad_gain = pl.pallas_call(
        add_halves,
        out_shape=(
            jax.ShapeDtypeStruct((4096, 128), BF16),
            jax.ShapeDtypeStruct((128, 512), BF16),
            jax.ShapeDtypeStruct((1, 128), F32),
        ),
        grid=(4,),
        in_specs=[quarter, quarter, value_block, gain_block],
        out_specs=(quarter, value_block, gain_block),
    )(own_out, other_out, grad_value, grad_gain)
    return grad_out[None], grad_value[None], grad_gain


def solution(mesh):
    return jax.shard_map(
        shards,
        mesh=mesh,
        in_specs=(
            P("pipe", "dp", "tensor"),
            P("pipe", "tensor"),
            P("pipe", ("tensor", "dp"), None),
            P("pipe", None, ("tensor", "dp")),
            P("pipe", "dp", None, "tensor", None, None),
            P("tensor"),
            P(),
            P("dp"),
            P("dp"),
        ),
        out_specs=(
            P("pipe", None, ("tensor", "dp")),
            P("pipe", ("tensor", "dp"), None),
            P("pipe", ("tensor", "dp")),
        ),
        check_vma=False,
    )
```

```python
import jax
import jax.numpy as jnp
from jax import lax
from jax.experimental import pallas as pl
from jax.experimental.pallas import tpu as pltpu
from jax.sharding import PartitionSpec as P

D = 8192
HD = 128
KVH = 4
EPS = 1e-05
F32 = jnp.float32
BF16 = jnp.bfloat16
MESH = pl.DeviceIdType.MESH
COPIES = 200
ORDER = (
    "mw",
    "maww",
    "m",
    "maw",
    "mwws",
    "maws",
    "mwws",
    "mw",
    "mbuu",
    "muu",
    "muubug",
    "mug",
    "mbg",
    "mubg",
    "moog",
    "mbougg",
    "mgoo",
    "mooq",
    "m",
    "moq",
    "mqqq",
    "mqqq",
    "m",
)


def dot(left, right):
    return jnp.dot(left, right, preferred_element_type=F32)


def split_pair(value):
    high = value.astype(BF16)
    return high, (value - high.astype(F32)).astype(BF16)


def kernel(
    score_ref, length_ref, return_ref, mask_ref, x_ref, gain_ref, wv_ref, w_ref, head_ref,
    go_own, go_in, gv_ref, gg_ref,
    att_own, att_all, v_all, x_other, xf, part, sum1, r0, r1, r2, r2x, gr_all,
    sq, sq_in, bm, att_t, v_bd, up_bd, wb, wq, wvb, wvt, gains, rms_all, hid, st, st_in,
    coef, ret, err_at, up, ng, vg, v_t, nrm_t, go_keep, go_send, gv_own, gv_send, gv_in,
    gg_own, gg_send, gg_in,
    send_sems, recv_sems, local_sems,
):
    pipe = lax.axis_index("pipe")
    tensor = lax.axis_index("tensor")
    dp = lax.axis_index("dp")
    c = lax.rem(tensor, 2)
    xh = lax.div(tensor, 2)
    z = lax.div(dp, 4)
    y = lax.rem(dp, 4)
    a = jnp.where(c == 0, z, y)
    b = jnp.where(c == 0, y, z)
    other = 1 - pipe

    def dp_of(a_at, b_at):
        return jnp.where(c == 0, a_at * 4 + b_at, b_at * 4 + a_at)

    core_peer = {"tensor": xh * 2 + 1 - c}
    x_tensor = (1 - xh) * 2 + c
    x_peer = {"tensor": x_tensor}
    pipe_peer = {"pipe": other}
    a_next = [lax.rem(a + k, 4) for k in (1, 2, 3)]
    b_next = [lax.rem(b + k, 4) for k in (1, 2, 3)]
    a_peers = [{"dp": dp_of(at, b)} for at in a_next]
    ax_peers = [{"dp": dp_of(at, b), "tensor": x_tensor} for at in [a] + a_next]
    b_peers = [{"dp": dp_of(a, bt)} for bt in b_next]
    t_peers = [{"tensor": lax.rem(tensor + k, 4)} for k in (1, 2, 3)]
    dp_next = [lax.rem(dp + k, 16) for k in range(16)]
    used = [0]

    def remote(src, dst, device):
        at = used[0]
        used[0] += 1
        return pltpu.make_async_remote_copy(
            src_ref=src, dst_ref=dst, send_sem=send_sems.at[at], recv_sem=recv_sems.at[at],
            device_id=device, device_id_type=MESH,
        )

    def start(copies):
        for one in copies:
            one.start()
        return copies

    def finish(copies):
        for one in copies:
            one.wait()

    def rows_of(first, size):
        return pl.ds(pl.multiple_of(first, size), size)

    loads = [
        pltpu.make_async_copy(wv_ref, wvb.at[pipe], local_sems.at[0]),
        pltpu.make_async_copy(w_ref, wb.at[pipe], local_sems.at[1]),
    ]
    start(loads)
    barrier = pltpu.get_barrier_semaphore()
    partners = [{"dp": to} for to in dp_next[1:]] + t_peers + ax_peers[1:] + [pipe_peer]
    for peer in partners:
        pl.semaphore_signal(barrier, inc=1, device_id=peer, device_id_type=MESH)
    pl.semaphore_wait(barrier, len(partners))

    def x_copies(rows, layer):
        return [
            remote(rows.at[:, rows_of(to * 128, 128)], xf.at[layer, rows_of(dp * 64, 64)], {"dp": to})
            for to in dp_next[1:]
        ]

    x_half = x_ref.at[rows_of(pipe * 64, 64)]
    x_cross = remote(x_ref.at[rows_of(other * 64, 64)], x_other, pipe_peer)
    x_own = x_copies(x_half, pipe)
    x_more = x_copies(x_other, other)
    square_copies = [
        [
            remote(sq.at[layer, lax.rem(peer["tensor"], 2)], sq_in.at[layer, tensor], peer)
            for peer in t_peers
        ]
        for layer in range(2)
    ]

    def send_x(layer, rows, copies):
        start(copies)
        xf[layer, rows_of(dp * 64, 64), :] = rows[:, rows_of(dp * 128, 128)]
        for m in range(2):
            block = rows[m * 32:(m + 1) * 32, :].astype(F32)
            sq[layer, m] = jnp.broadcast_to(jnp.sum(block * block, axis=1, keepdims=True), (32, 128))
        sq_in[layer, tensor] = sq[layer, c]
        start(square_copies[layer])

    def send_own_x(layer):
        @pl.when(pipe == layer)
        def _():
            send_x(layer, x_half, x_own)

    def send_other_x(layer):
        @pl.when(pipe != layer)
        def _():
            x_cross.wait_recv()
            send_x(layer, x_other, x_more)

    def wait_x(layer):
        @pl.when(pipe == layer)
        def _():
            finish(x_own)

        @pl.when(pipe != layer)
        def _():
            finish(x_more)

    att_cross = remote(att_own.at[other], att_all.at[pipe, c, a, b, xh], pipe_peer)

    def attend():
        row = lax.rem(lax.broadcasted_iota(jnp.int32, (256, 32), 0), 32)
        key = lax.broadcasted_iota(jnp.int32, (256, 32), 1)
        span = [length_ref[m, dp] for m in range(4)]
        weights = []
        for m in range(4):
            allowed = (key <= row) & (key < span[m])
            masked = jnp.where(allowed, score_ref[m].astype(F32).reshape(256, 32), -1e30)
            top = jnp.max(masked, axis=1, keepdims=True)
            exponent = jnp.where(allowed, jnp.exp(masked - top), 0.0)
            weights.append(exponent / jnp.sum(exponent, axis=1, keepdims=True))
        position = lax.broadcasted_iota(jnp.int32, (1, 128), 1)
        block = lax.div(position, 32)
        length = jnp.where(block == 0, span[0], span[1])
        length = jnp.where(block == 2, span[2], length)
        length = jnp.where(block == 3, span[3], length)
        live = ((lax.rem(position, 32) < length) & (mask_ref[...] == 1)).astype(F32)
        returns = return_ref[...]
        high = returns.astype(BF16).astype(F32)
        middle = (returns - high).astype(BF16).astype(F32)
        low = (returns - high - middle).astype(BF16).astype(F32)
        at = lax.broadcasted_iota(jnp.int32, (16, 128), 0)
        extra = jnp.where(at == 0, high, jnp.where(at == 1, middle, jnp.where(at == 2, low, 0.0)))
        extra = jnp.where(at == 3, live, extra).astype(BF16)
        for half in range(2):
            tile = [
                weights[half * 2 + m][q * 128:(q + 1) * 128] for q in range(2) for m in range(2)
            ]
            att_own[half, 0:128, :] = jnp.concatenate(tile, axis=1).astype(BF16)
            att_own[half, 128:144, :] = extra

    def gather_attention(layer):
        here = att_all.at[layer]

        @pl.when(pipe != layer)
        def _():
            att_cross.wait_recv()

        copies = start([remote(here.at[c, a, b, xh], here.at[c, a, b, xh], x_peer)])
        yield
        finish(copies)
        copies = start([remote(here.at[c, a, b], here.at[c, a, b], peer) for peer in a_peers])
        yield
        finish(copies)
        copies = start([remote(here.at[c, :, b], here.at[c, :, b], peer) for peer in b_peers])
        yield
        finish(copies)
        copies = start([remote(here.at[c], here.at[c], core_peer)])
        yield
        finish(copies)
        yield

    def scatter(layer, turn):
        here = part.at[layer]
        copies = start([remote(here.at[1 - c], r0.at[turn], core_peer)])
        yield
        finish(copies)

        def add0(at, carry):
            for bt in range(4):
                part[layer, c, at, bt] = (
                    part[layer, c, at, bt].astype(F32) + r0[turn, at, bt].astype(F32)
                ).astype(BF16)
            return carry

        lax.fori_loop(0, 4, add0, 0)
        copies = start([
            remote(here.at[c, :, bt], r1.at[turn, k], peer)
            for k, (bt, peer) in enumerate(zip(b_next, b_peers))
        ])
        yield
        finish(copies)
        for at in range(4):
            sum1[turn, at] = (
                part[layer, c, at, b].astype(F32) + r1[turn, 0, at].astype(F32)
                + r1[turn, 1, at].astype(F32) + r1[turn, 2, at].astype(F32)
            ).astype(BF16)
        copies = [
            remote(sum1.at[turn, at], r2x.at[turn, k], peer)
            for k, (at, peer) in enumerate(zip([a] + a_next, ax_peers))
        ]
        copies += [
            remote(sum1.at[turn, at], r2.at[turn, k], peer)
            for k, (at, peer) in enumerate(zip(a_next, a_peers))
        ]
        start(copies)
        yield
        finish(copies)

    def scattered(turn):
        total = sum1[turn, a].astype(F32)
        for k in range(3):
            total = total + r2[turn, k].astype(F32)
        for k in range(4):
            total = total + r2x[turn, k].astype(F32)
        return total

    def gather(here):
        copies = start([remote(here.at[c, a, b], here.at[c, a, b], peer) for peer in a_peers])
        yield
        finish(copies)
        copies = start([remote(here.at[c, :, b], here.at[c, :, b], peer) for peer in b_peers])
        yield
        finish(copies)
        copies = start([remote(here.at[c], here.at[c], core_peer)])
        yield
        finish(copies)

    heads = head_ref[...].astype(F32)
    head_at = lax.broadcasted_iota(jnp.int32, (16, 128), 0)
    head_row = jnp.sum(jnp.where(head_at == dp, heads, 0.0), axis=0, keepdims=True)
    lane = lax.broadcasted_iota(jnp.int32, (128, 128), 1)

    def project(layer):
        gain_row = gains[layer, 0:1, :]

        def body(zi, carry):
            xg = (xf[layer, rows_of(zi * 256, 256), :].astype(F32) * gain_row).astype(BF16)
            out = dot(xg, wvb[layer]).astype(BF16)
            for yi in range(4):
                part[layer, 0, zi, yi] = out[yi * 64:yi * 64 + 32]
                part[layer, 1, yi, zi] = out[yi * 64 + 32:yi * 64 + 64]
            return carry

        lax.fori_loop(0, 4, body, 0)

    def forward(layer):
        wait_x(layer)
        project(layer)
        yield from scatter(layer, layer)
        finish(square_copies[layer])
        squared = sq_in[layer, 0] + sq_in[layer, 1] + sq_in[layer, 2] + sq_in[layer, 3]
        rms = lax.rsqrt(squared / D + EPS)[:, 0:1]
        total = scattered(layer) * rms
        high, low = split_pair(rms)
        place = lax.broadcasted_iota(jnp.int32, (32, 128), 1)
        extra = jnp.where(place == 0, high.astype(F32), jnp.where(place == 1, low.astype(F32), 0.0))
        v_all[layer, c, a, b, :, 0:512] = total.astype(BF16)
        v_all[layer, c, a, b, :, 512:640] = extra.astype(BF16)
        yield from gather(v_all.at[layer])

    def mixture():
        def body(zi, carry):
            for yi in range(4):
                first = pl.multiple_of(zi * 256 + yi * 64, 64)
                for g in range(4):
                    places = (0, zi, yi) if g % 2 == 0 else (1, yi, zi)
                    att = att_all[(1, *places, g // 2)][0:128, :]
                    cols = slice(g * 128, (g + 1) * 128)
                    for m in range(2):
                        values = v_all[(1, 0, zi, yi) if m == 0 else (1, 1, yi, zi)][:, cols]
                        for q in range(2):
                            at = q * 2 + m
                            v_bd[yi, g, at * 32:(at + 1) * 32, at * 128:(at + 1) * 128] = values
                    out = dot(att, v_bd[yi, g]).astype(BF16)
                    for h in range(4):
                        for q in range(2):
                            for m in range(2):
                                head = g * 8 + q * 4 + h
                                bm[1, pl.ds(first + m * 32, 32), head * 128:(head + 1) * 128] = (
                                    out[h * 32:(h + 1) * 32, (q * 2 + m) * 128:(q * 2 + m + 1) * 128]
                                )
            return carry

        lax.fori_loop(0, 4, body, 0)

    def out_project():
        def body(k, carry):
            rows = rows_of(k * 512, 512)
            hid[rows, :] = xf[1, rows, :].astype(F32) + dot(bm[1, rows, :], wb[1])
            return carry

        lax.fori_loop(0, 2, body, 0)
        tile = jnp.zeros((128, 128), F32)
        for k in range(8):
            h = hid[k * 128:(k + 1) * 128, :]
            tile = jnp.where(lane == k, jnp.sum(h * h, axis=1, keepdims=True), tile)
            tile = jnp.where(lane == 8 + k, jnp.sum(h * head_row, axis=1, keepdims=True), tile)
        st[0] = tile.T[0:16]

    def targets():
        for d in range(16):
            extra = att_all[1, 0, d // 4, d % 4, 0, 128:144, :].astype(F32)
            at = 8 * (d % 2) + d // 2
            ret[at:at + 1, :] = extra[0:1] + extra[1:2] + extra[2:3]
            ret[16 + at:17 + at, :] = extra[3:4]
        returns = ret[0:16, :]
        live = ret[16:32, :]

        def whole(value):
            return jnp.sum(jnp.sum(value, axis=1, keepdims=True), axis=0, keepdims=True)

        count = jnp.maximum(whole(live), 1.0)
        mean = whole(live * returns) / count
        spread = whole(live * (returns - mean) * (returns - mean)) / count
        target = (returns - mean) * lax.rsqrt(spread + EPS)
        low = lax.broadcasted_iota(jnp.int32, (8, 128), 1) < 64
        for at, value in enumerate((target, live)):
            even, odd = value[0:8], value[8:16]
            err_at[0, at] = jnp.where(low, even, pltpu.roll(odd, 64, 1))
            err_at[1, at] = jnp.where(low, pltpu.roll(even, 64, 1), odd)

    def upstream(sums):
        target, live = err_at[pipe, 0], err_at[pipe, 1]
        out_scale = lax.rsqrt(sums[0:8] / D + EPS)
        critic = out_scale * sums[8:16]
        alpha = live * (critic - target) * out_scale
        beta = alpha * out_scale * critic / D
        coef[...] = jnp.concatenate([alpha, beta, jnp.zeros((112, 128), F32)], axis=0).T
        for k in range(8):
            rows = slice(k * 128, (k + 1) * 128)
            up[1, rows, :] = (
                coef[:, k:k + 1] * head_row - coef[:, 8 + k:9 + k] * hid[rows, :]
            ).astype(BF16)

    def turn_attention(layer):
        def body(zi, carry):
            for yi in range(4):
                for g in range(4):
                    places = (0, zi, yi) if g % 2 == 0 else (1, yi, zi)
                    turned = att_all[(layer, *places, g // 2)][0:128, :].T
                    for q in range(2):
                        for m in range(2):
                            att_t[layer, zi * 4 + yi, m, (g * 2 + q) * 32:(g * 2 + q + 1) * 32, :] = (
                                turned[(q * 2 + m) * 32:(q * 2 + m + 1) * 32]
                            )
            return carry

        lax.fori_loop(0, 4, body, 0)

    def prepare(layer):
        gain_row = gains[layer, 0:1, :]

        def body(zi, carry):
            for pair in range(2):
                first = pl.multiple_of(zi * 256 + pair * 128, 128)
                packets = []
                for yi in (pair * 2, pair * 2 + 1):
                    packets.append(v_all.at[layer, 0, zi, yi])
                    packets.append(v_all.at[layer, 1, yi, zi])
                extra = jnp.concatenate([one[:, 512:640] for one in packets], axis=0).astype(F32)
                rms = extra[:, 0:1] + extra[:, 1:2]
                rms_all[layer, pl.ds(first, 128), :] = jnp.broadcast_to(rms, (128, 128))
                normed = xf[layer, pl.ds(first, 128), :].astype(F32) * rms * gain_row
                nrm_t[layer, :, pl.ds(first, 128)] = normed.astype(BF16).T
                for g in range(4):
                    cols = slice(g * 128, (g + 1) * 128)
                    values = jnp.concatenate([one[:, cols] for one in packets], axis=0)
                    v_t[layer, g, :, pl.ds(first, 128)] = values.T
            return carry

        lax.fori_loop(0, 4, body, 0)

    def unmix(layer):
        def spread(d, carry):
            for m in range(2):
                first = pl.multiple_of(d * 64 + m * 32, 32)
                rows = up[layer, pl.ds(first, 32), :]
                for h in range(4):
                    up_bd[m, h * 32:(h + 1) * 32, h * 128:(h + 1) * 128] = rows
                out = dot(att_t[layer, d, m], up_bd[m]).astype(BF16)
                for q in range(8):
                    bm[layer, pl.ds(first, 32), q * 512:(q + 1) * 512] = out[q * 32:(q + 1) * 32, :]
            return carry

        lax.fori_loop(0, 16, spread, 0)

        def body(k, carry):
            rows = rows_of(k * 512, 512)
            for g in range(4):
                cols = slice(g * 1024, (g + 1) * 1024)
                out = dot(bm[layer, rows, cols], wq[layer, cols, :]).astype(BF16)
                for zi in range(2):
                    for yi in range(4):
                        first = zi * 256 + yi * 64
                        into = slice(g * 128, (g + 1) * 128)
                        part[layer, 0, k * 2 + zi, yi, :, into] = out[first:first + 32]
                        part[layer, 1, yi, k * 2 + zi, :, into] = out[first + 32:first + 64]
            return carry

        lax.fori_loop(0, 2, body, 0)

    def norm_back(layer):
        def body(zi, carry):
            first = pl.multiple_of(zi * 256, 256)
            for yi in range(4):
                vg[layer, pl.ds(first + yi * 64, 32), :] = gr_all[layer, 0, zi, yi]
                vg[layer, pl.ds(first + yi * 64 + 32, 32), :] = gr_all[layer, 1, yi, zi]
            ng[layer, pl.ds(first, 256), :] = dot(vg[layer, pl.ds(first, 256), :], wvt[layer])
            return carry

        lax.fori_loop(0, 4, body, 0)

    def input_grad(layer):
        gain_row = gains[layer, 0:1, :]

        def body(zi, carry):
            for yi in range(4):
                for m in range(2):
                    rows = pl.ds(pl.multiple_of(zi * 256 + yi * 64 + m * 32, 32), 32)
                    values = v_all[(layer, 0, zi, yi) if m == 0 else (layer, 1, yi, zi)][:, 0:512]
                    product = vg[layer, rows, :].astype(F32) * values.astype(F32)
                    inner = jnp.sum(product, axis=1, keepdims=True)
                    rms = rms_all[layer, rows, :]
                    up[layer - 1, rows, :] = (
                        up[layer, rows, :].astype(F32) + rms * gain_row * ng[layer, rows, :]
                        - (rms * rms * (inner / D)) * xf[layer, rows, :].astype(F32)
                    ).astype(BF16)
            return carry

        lax.fori_loop(0, 4, body, 0)

    go_copies = [
        remote(go_send.at[k * 512:(k + 1) * 512], go_in.at[k * 512:(k + 1) * 512], pipe_peer)
        for k in range(8)
    ]
    keep = pltpu.make_async_copy(go_keep, go_own, local_sems.at[2])
    gv_copy = remote(gv_send, gv_in, pipe_peer)
    gg_copy = remote(gg_send, gg_in, pipe_peer)

    def out_grad(layer):
        for g in range(4):
            def body(k, carry):
                out = dot(v_t[layer, g], bm[layer, :, rows_of(g * 1024 + k * 512, 512)])

                @pl.when(pipe == layer)
                def _():
                    for h in range(4):
                        go_keep[rows_of(g * 1024 + k * 512 + h * 128, 128), :] = (
                            out[:, h * 128:(h + 1) * 128].astype(BF16)
                        )

                @pl.when(pipe != layer)
                def _():
                    for h in range(4):
                        go_send[rows_of(g * 1024 + k * 512 + h * 128, 128), :] = (
                            out[:, h * 128:(h + 1) * 128].astype(BF16)
                        )

                return carry

            lax.fori_loop(0, 2, body, 0)

        @pl.when(pipe == layer)
        def _():
            keep.start()

    def small_grads(layer):
        def value_grad(k, total):
            cols = rows_of(k * 256, 256)
            return total + dot(nrm_t[layer, :, cols], vg[layer, cols, :])

        value_total = lax.fori_loop(0, 4, value_grad, jnp.zeros((128, 512), F32))

        def gain_grad(k, total):
            rows = rows_of(k * 128, 128)
            gained = ng[layer, rows, :] * xf[layer, rows, :].astype(F32) * rms_all[layer, rows, :]
            return total + jnp.sum(gained.reshape(16, 8, 128), axis=0)

        gain_total = lax.fori_loop(0, 8, gain_grad, jnp.zeros((8, 128), F32))

        @pl.when(pipe == layer)
        def _():
            gv_own[...] = value_total
            gg_own[...] = gain_total

        @pl.when(pipe != layer)
        def _():
            gv_send[...] = value_total.astype(BF16)
            gg_send[...] = gain_total
            gv_copy.start()
            gg_copy.start()

    def sum_up(copies, peers, at):
        for one in copies:
            one.wait()
        st[at + 1] = st[at] + st_in[at, 0] + st_in[at, 1] + st_in[at, 2]

    def main():
        yield from forward(1)
        mixture()
        yield
        out_project()
        copies = start([remote(st.at[0], st_in.at[0, k], peer) for k, peer in enumerate(t_peers)])
        yield
        turn_attention(1)
        targets()
        sum_up(copies, t_peers, 0)
        copies = start([remote(st.at[1], st_in.at[1, k], peer) for k, peer in enumerate(b_peers)])
        yield
        prepare(1)
        sum_up(copies, b_peers, 1)
        copies = start([remote(st.at[2], st_in.at[2, k], peer) for k, peer in enumerate(a_peers)])
        yield
        sum_up(copies, a_peers, 2)
        upstream(st[3])
        for layer in (1, 0):
            unmix(layer)
            turn = 2 + layer
            steps = scatter(layer, turn)
            next(steps)
            yield
            next(steps)
            out_grad(layer)
            yield
            yield from steps
            gr_all[layer, c, a, b] = scattered(turn).astype(BF16)
            steps = gather(gr_all.at[layer])
            next(steps)
            yield
            next(steps)
            if layer == 0:
                small_grads(1)
            yield
            yield from steps
            norm_back(layer)
            if layer == 1:
                input_grad(1)
        small_grads(0)
        yield

    def background():
        yield from forward(0)
        turn_attention(0)
        yield
        prepare(0)
        yield

    @pl.when(pipe == 1)
    def _():
        x_cross.start()

    gains[pipe, 0:8, :] = jnp.broadcast_to(gain_ref[:, rows_of(dp * 128, 128)], (8, 128))
    loads[0].wait()
    cross = start([
        remote(gains.at[pipe], gains.at[pipe], pipe_peer),
        remote(wvb.at[pipe], wvb.at[pipe], pipe_peer),
    ])
    send_own_x(1)
    attend()
    att_cross.start()
    att_all[pipe, c, a, b, xh] = att_own[pipe]
    send_other_x(1)
    attention1 = gather_attention(1)
    next(attention1)
    loads[1].wait()

    def turn_w(layer):
        def body(k, carry):
            wq[layer, rows_of(k * 128, 128), :] = wb[layer, rows_of(k * 128, 128), :].T
            return carry

        lax.fori_loop(0, 32, body, 0)
        for k in range(4):
            wvt[layer, k * 128:(k + 1) * 128, :] = wvb[layer, :, k * 128:(k + 1) * 128].T

    v_bd[...] = jnp.zeros_like(v_bd)
    up_bd[...] = jnp.zeros_like(up_bd)
    finish(cross)
    next(attention1)

    @pl.when(pipe == 1)
    def _():
        att_cross.wait_send()

    w_copies = [
        remote(wb.at[pipe, k * 512:(k + 1) * 512], wb.at[pipe, k * 512:(k + 1) * 512], pipe_peer)
        for k in range(8)
    ]

    def pieces(copies, sender):
        for one in copies:
            @pl.when(pipe == sender)
            def _():
                one.start()

            yield

    def weights(layer):
        for _ in pieces(w_copies, layer):
            yield
        for one in w_copies:
            @pl.when(pipe == layer)
            def _():
                one.wait_send()

            @pl.when(pipe != layer)
            def _():
                one.wait_recv()

        yield
        turn_w(layer)
        yield

    def other_x():
        @pl.when(pipe == 0)
        def _():
            x_cross.start()

        yield
        send_own_x(0)
        yield
        send_other_x(0)
        yield

    streams = {
        "m": main(), "g": background(), "a": attention1, "b": gather_attention(0),
        "w": weights(1), "u": weights(0), "s": other_x(),
        "o": pieces(go_copies, 0), "q": pieces(go_copies, 1),
    }
    for names in ORDER:
        for name in names:
            next(streams[name])

    @pl.when(pipe == 0)
    def _():
        att_cross.wait_send()

    x_cross.wait_send()

    for one in go_copies:
        one.wait()
    keep.wait()
    gv_copy.wait()
    gg_copy.wait()
    gv_ref[...] = (gv_own[...] + gv_in[...].astype(F32)).astype(BF16)
    gg_ref[...] = jnp.sum(gg_own[...] + gg_in[...], axis=0, keepdims=True)


def add_halves(own_ref, other_ref, value_ref, gain_ref, go_ref, gv_ref, gg_ref):
    go_ref[...] = (own_ref[...].astype(F32) + other_ref[...].astype(F32)).astype(BF16)

    @pl.when(pl.program_id(0) == 0)
    def _():
        gv_ref[...] = value_ref[...]
        gg_ref[...] = gain_ref[...]


def shards(
    layer_inputs, norm_gain, value_weight, out_weight, scores, head_weight, lengths, returns,
    response_mask,
):
    vmem = pl.BlockSpec(memory_space=pltpu.VMEM)
    anywhere = pl.BlockSpec(memory_space=pl.ANY)
    smem = pl.BlockSpec(memory_space=pltpu.SMEM)

    def scratch(*shape, dtype=BF16):
        return pltpu.VMEM(shape, dtype)

    own_out, other_out, grad_value, grad_gain = pl.pallas_call(
        kernel,
        out_shape=(
            jax.ShapeDtypeStruct((4096, 128), BF16),
            jax.ShapeDtypeStruct((4096, 128), BF16),
            jax.ShapeDtypeStruct((128, 512), BF16),
            jax.ShapeDtypeStruct((1, 128), F32),
        ),
        in_specs=[vmem, smem, vmem, vmem, vmem, vmem, anywhere, anywhere, vmem],
        out_specs=(anywhere, anywhere, vmem, vmem),
        scratch_shapes=[
            scratch(2, 144, 128),
            scratch(2, 2, 4, 4, 2, 144, 128),
            scratch(2, 2, 4, 4, 32, 640),
            scratch(64, 2048),
            scratch(2, 1024, 128),
            scratch(2, 2, 4, 4, 32, 512),
            scratch(4, 4, 32, 512),
            scratch(4, 4, 4, 32, 512),
            scratch(4, 3, 4, 32, 512),
            scratch(4, 3, 32, 512),
            scratch(4, 4, 32, 512),
            scratch(2, 2, 4, 4, 32, 512),
            scratch(2, 2, 32, 128, dtype=F32),
            scratch(2, 4, 32, 128, dtype=F32),
            scratch(2, 1024, 4096),
            scratch(2, 16, 2, 256, 128),
            scratch(4, 4, 128, 512),
            scratch(2, 128, 512),
            scratch(2, 4096, 128),
            scratch(2, 4096, 128),
            scratch(2, 128, 512),
            scratch(2, 512, 128),
            scratch(2, 8, 128, dtype=F32),
            scratch(2, 1024, 128, dtype=F32),
            scratch(1024, 128, dtype=F32),
            scratch(4, 16, 128, dtype=F32),
            scratch(3, 3, 16, 128, dtype=F32),
            scratch(128, 128, dtype=F32),
            scratch(32, 128, dtype=F32),
            scratch(2, 2, 8, 128, dtype=F32),
            scratch(2, 1024, 128),
            scratch(2, 1024, 128, dtype=F32),
            scratch(2, 1024, 512),
            scratch(2, 4, 128, 1024),
            scratch(2, 128, 1024),
            scratch(4096, 128),
            scratch(4096, 128),
            scratch(128, 512, dtype=F32),
            scratch(128, 512),
            scratch(128, 512),
            scratch(8, 128, dtype=F32),
            scratch(8, 128, dtype=F32),
            scratch(8, 128, dtype=F32),
            pltpu.SemaphoreType.DMA((COPIES,)),
            pltpu.SemaphoreType.DMA((COPIES,)),
            pltpu.SemaphoreType.DMA((3,)),
        ],
        compiler_params=pltpu.CompilerParams(
            collective_id=0, has_side_effects=True, vmem_limit_bytes=60 * 1024 * 1024
        ),
        cost_estimate=pl.CostEstimate(
            flops=8_000_000_000, bytes_accessed=6_000_000, transcendentals=0
        ),
    )(
        scores[0, 0],
        lengths.T,
        returns.reshape(1, 128),
        response_mask.reshape(1, 128),
        layer_inputs[0],
        norm_gain,
        value_weight[0],
        out_weight[0],
        head_weight.reshape(16, 128),
    )
    quarter = pl.BlockSpec((1024, 128), lambda k: (k, 0))
    value_block = pl.BlockSpec((128, 512), lambda k: (0, 0))
    gain_block = pl.BlockSpec((1, 128), lambda k: (0, 0))
    grad_out, grad_value, grad_gain = pl.pallas_call(
        add_halves,
        out_shape=(
            jax.ShapeDtypeStruct((4096, 128), BF16),
            jax.ShapeDtypeStruct((128, 512), BF16),
            jax.ShapeDtypeStruct((1, 128), F32),
        ),
        grid=(4,),
        in_specs=[quarter, quarter, value_block, gain_block],
        out_specs=(quarter, value_block, gain_block),
    )(own_out, other_out, grad_value, grad_gain)
    return grad_out[None], grad_value[None], grad_gain


def solution(mesh):
    return jax.shard_map(
        shards,
        mesh=mesh,
        in_specs=(
            P("pipe", "dp", "tensor"),
            P("pipe", "tensor"),
            P("pipe", ("tensor", "dp"), None),
            P("pipe", None, ("tensor", "dp")),
            P("pipe", "dp", None, "tensor", None, None),
            P("tensor"),
            P(),
            P("dp"),
            P("dp"),
        ),
        out_specs=(
            P("pipe", None, ("tensor", "dp")),
            P("pipe", ("tensor", "dp"), None),
            P("pipe", ("tensor", "dp")),
        ),
        check_vma=False,
    )
```

```python
import jax
import jax.numpy as jnp
from jax import lax
from jax.experimental import pallas as pl
from jax.experimental.pallas import tpu as pltpu
from jax.sharding import PartitionSpec as P

D = 8192
HD = 128
KVH = 4
EPS = 1e-05
F32 = jnp.float32
BF16 = jnp.bfloat16
MESH = pl.DeviceIdType.MESH
COPIES = 200
ORDER = (
    "mw",
    "maww",
    "m",
    "maw",
    "mww",
    "maws",
    "mww",
    "mw",
    "mbuu",
    "muug",
    "muubug",
    "mug",
    "mbg",
    "mubg",
    "moog",
    "mboug",
    "mgoo",
    "mooq",
    "m",
    "moq",
    "mqqq",
    "mqqq",
    "m",
)


def dot(left, right):
    return jnp.dot(left, right, preferred_element_type=F32)


def split_pair(value):
    high = value.astype(BF16)
    return high, (value - high.astype(F32)).astype(BF16)


def kernel(
    score_ref, length_ref, return_ref, mask_ref, x_ref, gain_ref, wv_ref, w_ref, head_ref,
    go_own, go_in, gv_ref, gg_ref,
    att_own, att_all, v_all, xf, part, sum1, r0, r1, r2, r2x, gr_all,
    sq, sq_in, bm, att_t, v_bd, up_bd, wb, wq, wvb, wvt, gains, rms_own, rms_all, hid, st, st_in,
    coef, ret, err_at, up, ng, vg, v_t, nrm_t, go_keep, go_send, gv_own, gv_send, gv_in,
    gg_own, gg_send, gg_in,
    send_sems, recv_sems, local_sems,
):
    pipe = lax.axis_index("pipe")
    tensor = lax.axis_index("tensor")
    dp = lax.axis_index("dp")
    c = lax.rem(tensor, 2)
    xh = lax.div(tensor, 2)
    z = lax.div(dp, 4)
    y = lax.rem(dp, 4)
    a = jnp.where(c == 0, z, y)
    b = jnp.where(c == 0, y, z)
    other = 1 - pipe

    def dp_of(a_at, b_at):
        return jnp.where(c == 0, a_at * 4 + b_at, b_at * 4 + a_at)

    core_peer = {"tensor": xh * 2 + 1 - c}
    x_tensor = (1 - xh) * 2 + c
    x_peer = {"tensor": x_tensor}
    pipe_peer = {"pipe": other}
    a_next = [lax.rem(a + k, 4) for k in (1, 2, 3)]
    b_next = [lax.rem(b + k, 4) for k in (1, 2, 3)]
    a_peers = [{"dp": dp_of(at, b)} for at in a_next]
    ax_peers = [{"dp": dp_of(at, b), "tensor": x_tensor} for at in [a] + a_next]
    b_peers = [{"dp": dp_of(a, bt)} for bt in b_next]
    t_peers = [{"tensor": lax.rem(tensor + k, 4)} for k in (1, 2, 3)]
    dp_next = [lax.rem(dp + k, 16) for k in range(16)]
    used = [0]

    def remote(src, dst, device):
        at = used[0]
        used[0] += 1
        return pltpu.make_async_remote_copy(
            src_ref=src, dst_ref=dst, send_sem=send_sems.at[at], recv_sem=recv_sems.at[at],
            device_id=device, device_id_type=MESH,
        )

    def start(copies):
        for one in copies:
            one.start()
        return copies

    def finish(copies):
        for one in copies:
            one.wait()

    def rows_of(first, size):
        return pl.ds(pl.multiple_of(first, size), size)

    loads = [
        pltpu.make_async_copy(wv_ref, wvb.at[pipe], local_sems.at[0]),
        pltpu.make_async_copy(w_ref, wb.at[pipe], local_sems.at[1]),
    ]
    start(loads)
    barrier = pltpu.get_barrier_semaphore()
    partners = [{"dp": to} for to in dp_next[1:]] + t_peers + ax_peers[1:]
    partners += [{"dp": to, "pipe": other} for to in dp_next]
    partners += [{"tensor": one["tensor"], "pipe": other} for one in t_peers]
    for peer in partners:
        pl.semaphore_signal(barrier, inc=1, device_id=peer, device_id_type=MESH)
    pl.semaphore_wait(barrier, len(partners))

    def x_copy(to, device, half):
        return remote(
            x_ref.at[rows_of(half * 64, 64), rows_of(to * 128, 128)],
            xf.at[pipe, rows_of(dp * 64, 64)], device,
        )

    x_same = [x_copy(to, {"dp": to}, pipe) for to in dp_next[1:]]
    x_cross = [x_copy(to, {"dp": to, "pipe": other}, other) for to in dp_next]

    def send_x(layer):
        @pl.when(pipe == layer)
        def _():
            start(x_cross)
            start(x_same)
            xf[layer, rows_of(dp * 64, 64), :] = x_ref[rows_of(layer * 64, 64), rows_of(dp * 128, 128)]

    def wait_x(layer):
        @pl.when(pipe == layer)
        def _():
            finish(x_same)
            for one in x_cross:
                one.wait_send()

        @pl.when(pipe != layer)
        def _():
            for one in x_cross:
                one.wait_recv()

    att_cross = remote(att_own.at[other], att_all.at[pipe, c, a, b, xh], pipe_peer)

    def attend():
        row = lax.rem(lax.broadcasted_iota(jnp.int32, (256, 32), 0), 32)
        key = lax.broadcasted_iota(jnp.int32, (256, 32), 1)
        span = [length_ref[m, dp] for m in range(4)]
        weights = []
        for m in range(4):
            allowed = (key <= row) & (key < span[m])
            masked = jnp.where(allowed, score_ref[m].astype(F32).reshape(256, 32), -1e30)
            top = jnp.max(masked, axis=1, keepdims=True)
            exponent = jnp.where(allowed, jnp.exp(masked - top), 0.0)
            weights.append(exponent / jnp.sum(exponent, axis=1, keepdims=True))
        position = lax.broadcasted_iota(jnp.int32, (1, 128), 1)
        block = lax.div(position, 32)
        length = jnp.where(block == 0, span[0], span[1])
        length = jnp.where(block == 2, span[2], length)
        length = jnp.where(block == 3, span[3], length)
        live = ((lax.rem(position, 32) < length) & (mask_ref[...] == 1)).astype(F32)
        returns = return_ref[...]
        high = returns.astype(BF16).astype(F32)
        middle = (returns - high).astype(BF16).astype(F32)
        low = (returns - high - middle).astype(BF16).astype(F32)
        at = lax.broadcasted_iota(jnp.int32, (16, 128), 0)
        extra = jnp.where(at == 0, high, jnp.where(at == 1, middle, jnp.where(at == 2, low, 0.0)))
        extra = jnp.where(at == 3, live, extra).astype(BF16)
        for half in range(2):
            tile = [
                weights[half * 2 + m][q * 128:(q + 1) * 128] for q in range(2) for m in range(2)
            ]
            att_own[half, 0:128, :] = jnp.concatenate(tile, axis=1).astype(BF16)
            att_own[half, 128:144, :] = extra

    def gather_attention(layer):
        here = att_all.at[layer]

        @pl.when(pipe != layer)
        def _():
            att_cross.wait_recv()

        copies = start([remote(here.at[c, a, b, xh], here.at[c, a, b, xh], x_peer)])
        yield
        finish(copies)
        copies = start([remote(here.at[c, a, b], here.at[c, a, b], peer) for peer in a_peers])
        yield
        finish(copies)
        copies = start([remote(here.at[c, :, b], here.at[c, :, b], peer) for peer in b_peers])
        yield
        finish(copies)
        copies = start([remote(here.at[c], here.at[c], core_peer)])
        yield
        finish(copies)
        yield

    def scatter(layer, turn):
        here = part.at[layer]
        copies = start([remote(here.at[1 - c], r0.at[turn], core_peer)])
        yield
        finish(copies)

        def add0(at, carry):
            for bt in range(4):
                part[layer, c, at, bt] = (
                    part[layer, c, at, bt].astype(F32) + r0[turn, at, bt].astype(F32)
                ).astype(BF16)
            return carry

        lax.fori_loop(0, 4, add0, 0)
        copies = start([
            remote(here.at[c, :, bt], r1.at[turn, k], peer)
            for k, (bt, peer) in enumerate(zip(b_next, b_peers))
        ])
        yield
        finish(copies)
        for at in range(4):
            sum1[turn, at] = (
                part[layer, c, at, b].astype(F32) + r1[turn, 0, at].astype(F32)
                + r1[turn, 1, at].astype(F32) + r1[turn, 2, at].astype(F32)
            ).astype(BF16)
        copies = [
            remote(sum1.at[turn, at], r2x.at[turn, k], peer)
            for k, (at, peer) in enumerate(zip([a] + a_next, ax_peers))
        ]
        copies += [
            remote(sum1.at[turn, at], r2.at[turn, k], peer)
            for k, (at, peer) in enumerate(zip(a_next, a_peers))
        ]
        start(copies)
        yield
        finish(copies)

    def scattered(turn):
        total = sum1[turn, a].astype(F32)
        for k in range(3):
            total = total + r2[turn, k].astype(F32)
        for k in range(4):
            total = total + r2x[turn, k].astype(F32)
        return total

    def gather(here):
        copies = start([remote(here.at[c, a, b], here.at[c, a, b], peer) for peer in a_peers])
        yield
        finish(copies)
        copies = start([remote(here.at[c, :, b], here.at[c, :, b], peer) for peer in b_peers])
        yield
        finish(copies)
        copies = start([remote(here.at[c], here.at[c], core_peer)])
        yield
        finish(copies)

    heads = head_ref[...].astype(F32)
    head_at = lax.broadcasted_iota(jnp.int32, (16, 128), 0)
    head_row = jnp.sum(jnp.where(head_at == dp, heads, 0.0), axis=0, keepdims=True)
    lane = lax.broadcasted_iota(jnp.int32, (128, 128), 1)

    def project(layer):
        gain_row = gains[layer, 0:1, :]

        def body(zi, carry):
            xg = (xf[layer, rows_of(zi * 256, 256), :].astype(F32) * gain_row).astype(BF16)
            out = dot(xg, wvb[layer]).astype(BF16)
            for yi in range(4):
                part[layer, 0, zi, yi] = out[yi * 64:yi * 64 + 32]
                part[layer, 1, yi, zi] = out[yi * 64 + 32:yi * 64 + 64]
            return carry

        lax.fori_loop(0, 4, body, 0)

    def forward(layer):
        wait_x(layer)
        project(layer)
        yield from scatter(layer, layer)
        rms = rms_own[layer, :, 0:1]
        total = scattered(layer) * rms
        high, low = split_pair(rms)
        place = lax.broadcasted_iota(jnp.int32, (32, 128), 1)
        extra = jnp.where(place == 0, high.astype(F32), jnp.where(place == 1, low.astype(F32), 0.0))
        v_all[layer, c, a, b, :, 0:512] = total.astype(BF16)
        v_all[layer, c, a, b, :, 512:640] = extra.astype(BF16)
        yield from gather(v_all.at[layer])

    def mixture():
        def body(zi, carry):
            for yi in range(4):
                first = pl.multiple_of(zi * 256 + yi * 64, 64)
                for g in range(4):
                    places = (0, zi, yi) if g % 2 == 0 else (1, yi, zi)
                    att = att_all[(1, *places, g // 2)][0:128, :]
                    cols = slice(g * 128, (g + 1) * 128)
                    for m in range(2):
                        values = v_all[(1, 0, zi, yi) if m == 0 else (1, 1, yi, zi)][:, cols]
                        for q in range(2):
                            at = q * 2 + m
                            v_bd[yi, g, at * 32:(at + 1) * 32, at * 128:(at + 1) * 128] = values
                    out = dot(att, v_bd[yi, g]).astype(BF16)
                    for h in range(4):
                        for q in range(2):
                            for m in range(2):
                                head = g * 8 + q * 4 + h
                                bm[1, pl.ds(first + m * 32, 32), head * 128:(head + 1) * 128] = (
                                    out[h * 32:(h + 1) * 32, (q * 2 + m) * 128:(q * 2 + m + 1) * 128]
                                )
            return carry

        lax.fori_loop(0, 4, body, 0)

    def out_project():
        def body(k, carry):
            rows = rows_of(k * 512, 512)
            hid[rows, :] = xf[1, rows, :].astype(F32) + dot(bm[1, rows, :], wb[1])
            return carry

        lax.fori_loop(0, 2, body, 0)
        tile = jnp.zeros((128, 128), F32)
        for k in range(8):
            h = hid[k * 128:(k + 1) * 128, :]
            tile = jnp.where(lane == k, jnp.sum(h * h, axis=1, keepdims=True), tile)
            tile = jnp.where(lane == 8 + k, jnp.sum(h * head_row, axis=1, keepdims=True), tile)
        st[0] = tile.T[0:16]

    def targets():
        for d in range(16):
            extra = att_all[1, 0, d // 4, d % 4, 0, 128:144, :].astype(F32)
            at = 8 * (d % 2) + d // 2
            ret[at:at + 1, :] = extra[0:1] + extra[1:2] + extra[2:3]
            ret[16 + at:17 + at, :] = extra[3:4]
        returns = ret[0:16, :]
        live = ret[16:32, :]

        def whole(value):
            return jnp.sum(jnp.sum(value, axis=1, keepdims=True), axis=0, keepdims=True)

        count = jnp.maximum(whole(live), 1.0)
        mean = whole(live * returns) / count
        spread = whole(live * (returns - mean) * (returns - mean)) / count
        target = (returns - mean) * lax.rsqrt(spread + EPS)
        low = lax.broadcasted_iota(jnp.int32, (8, 128), 1) < 64
        for at, value in enumerate((target, live)):
            even, odd = value[0:8], value[8:16]
            err_at[0, at] = jnp.where(low, even, pltpu.roll(odd, 64, 1))
            err_at[1, at] = jnp.where(low, pltpu.roll(even, 64, 1), odd)

    def upstream(sums):
        target, live = err_at[pipe, 0], err_at[pipe, 1]
        out_scale = lax.rsqrt(sums[0:8] / D + EPS)
        critic = out_scale * sums[8:16]
        alpha = live * (critic - target) * out_scale
        beta = alpha * out_scale * critic / D
        coef[...] = jnp.concatenate([alpha, beta, jnp.zeros((112, 128), F32)], axis=0).T
        for k in range(8):
            rows = slice(k * 128, (k + 1) * 128)
            up[1, rows, :] = (
                coef[:, k:k + 1] * head_row - coef[:, 8 + k:9 + k] * hid[rows, :]
            ).astype(BF16)

    def turn_attention(layer):
        def body(zi, carry):
            for yi in range(4):
                for g in range(4):
                    places = (0, zi, yi) if g % 2 == 0 else (1, yi, zi)
                    turned = att_all[(layer, *places, g // 2)][0:128, :].T
                    for q in range(2):
                        for m in range(2):
                            att_t[layer, zi * 4 + yi, m, (g * 2 + q) * 32:(g * 2 + q + 1) * 32, :] = (
                                turned[(q * 2 + m) * 32:(q * 2 + m + 1) * 32]
                            )
            return carry

        lax.fori_loop(0, 4, body, 0)

    def prepare(layer):
        gain_row = gains[layer, 0:1, :]

        def body(zi, carry):
            for pair in range(2):
                first = pl.multiple_of(zi * 256 + pair * 128, 128)
                packets = []
                for yi in (pair * 2, pair * 2 + 1):
                    packets.append(v_all.at[layer, 0, zi, yi])
                    packets.append(v_all.at[layer, 1, yi, zi])
                extra = jnp.concatenate([one[:, 512:640] for one in packets], axis=0).astype(F32)
                rms = extra[:, 0:1] + extra[:, 1:2]
                rms_all[layer, pl.ds(first, 128), :] = jnp.broadcast_to(rms, (128, 128))
                normed = xf[layer, pl.ds(first, 128), :].astype(F32) * rms * gain_row
                nrm_t[layer, :, pl.ds(first, 128)] = normed.astype(BF16).T
                for g in range(4):
                    cols = slice(g * 128, (g + 1) * 128)
                    values = jnp.concatenate([one[:, cols] for one in packets], axis=0)
                    v_t[layer, g, :, pl.ds(first, 128)] = values.T
            return carry

        lax.fori_loop(0, 4, body, 0)

    def unmix(layer):
        def spread(d, carry):
            for m in range(2):
                first = pl.multiple_of(d * 64 + m * 32, 32)
                rows = up[layer, pl.ds(first, 32), :]
                for h in range(4):
                    up_bd[m, h * 32:(h + 1) * 32, h * 128:(h + 1) * 128] = rows
                out = dot(att_t[layer, d, m], up_bd[m]).astype(BF16)
                for q in range(8):
                    bm[layer, pl.ds(first, 32), q * 512:(q + 1) * 512] = out[q * 32:(q + 1) * 32, :]
            return carry

        lax.fori_loop(0, 16, spread, 0)

        def body(k, carry):
            rows = rows_of(k * 512, 512)
            for g in range(4):
                cols = slice(g * 1024, (g + 1) * 1024)
                out = dot(bm[layer, rows, cols], wq[layer, cols, :]).astype(BF16)
                for zi in range(2):
                    for yi in range(4):
                        first = zi * 256 + yi * 64
                        into = slice(g * 128, (g + 1) * 128)
                        part[layer, 0, k * 2 + zi, yi, :, into] = out[first:first + 32]
                        part[layer, 1, yi, k * 2 + zi, :, into] = out[first + 32:first + 64]
            return carry

        lax.fori_loop(0, 2, body, 0)

    def norm_back(layer):
        def body(zi, carry):
            first = pl.multiple_of(zi * 256, 256)
            for yi in range(4):
                vg[layer, pl.ds(first + yi * 64, 32), :] = gr_all[layer, 0, zi, yi]
                vg[layer, pl.ds(first + yi * 64 + 32, 32), :] = gr_all[layer, 1, yi, zi]
            ng[layer, pl.ds(first, 256), :] = dot(vg[layer, pl.ds(first, 256), :], wvt[layer])
            return carry

        lax.fori_loop(0, 4, body, 0)

    def input_grad(layer):
        gain_row = gains[layer, 0:1, :]

        def body(zi, carry):
            for yi in range(4):
                for m in range(2):
                    rows = pl.ds(pl.multiple_of(zi * 256 + yi * 64 + m * 32, 32), 32)
                    values = v_all[(layer, 0, zi, yi) if m == 0 else (layer, 1, yi, zi)][:, 0:512]
                    product = vg[layer, rows, :].astype(F32) * values.astype(F32)
                    inner = jnp.sum(product, axis=1, keepdims=True)
                    rms = rms_all[layer, rows, :]
                    up[layer - 1, rows, :] = (
                        up[layer, rows, :].astype(F32) + rms * gain_row * ng[layer, rows, :]
                        - (rms * rms * (inner / D)) * xf[layer, rows, :].astype(F32)
                    ).astype(BF16)
            return carry

        lax.fori_loop(0, 4, body, 0)

    go_copies = [
        remote(go_send.at[k * 512:(k + 1) * 512], go_in.at[k * 512:(k + 1) * 512], pipe_peer)
        for k in range(8)
    ]
    keep = pltpu.make_async_copy(go_keep, go_own, local_sems.at[2])
    gv_copy = remote(gv_send, gv_in, pipe_peer)
    gg_copy = remote(gg_send, gg_in, pipe_peer)

    def out_grad(layer):
        for g in range(4):
            def body(k, carry):
                out = dot(v_t[layer, g], bm[layer, :, rows_of(g * 1024 + k * 512, 512)])

                @pl.when(pipe == layer)
                def _():
                    for h in range(4):
                        go_keep[rows_of(g * 1024 + k * 512 + h * 128, 128), :] = (
                            out[:, h * 128:(h + 1) * 128].astype(BF16)
                        )

                @pl.when(pipe != layer)
                def _():
                    for h in range(4):
                        go_send[rows_of(g * 1024 + k * 512 + h * 128, 128), :] = (
                            out[:, h * 128:(h + 1) * 128].astype(BF16)
                        )

                return carry

            lax.fori_loop(0, 2, body, 0)

        @pl.when(pipe == layer)
        def _():
            keep.start()

    def small_grads(layer):
        def value_grad(k, total):
            cols = rows_of(k * 256, 256)
            return total + dot(nrm_t[layer, :, cols], vg[layer, cols, :])

        value_total = lax.fori_loop(0, 4, value_grad, jnp.zeros((128, 512), F32))

        def gain_grad(k, total):
            rows = rows_of(k * 128, 128)
            gained = ng[layer, rows, :] * xf[layer, rows, :].astype(F32) * rms_all[layer, rows, :]
            return total + jnp.sum(gained.reshape(16, 8, 128), axis=0)

        gain_total = lax.fori_loop(0, 8, gain_grad, jnp.zeros((8, 128), F32))

        @pl.when(pipe == layer)
        def _():
            gv_own[...] = value_total
            gg_own[...] = gain_total

        @pl.when(pipe != layer)
        def _():
            gv_send[...] = value_total.astype(BF16)
            gg_send[...] = gain_total
            gv_copy.start()
            gg_copy.start()

    def sum_up(copies, peers, at):
        for one in copies:
            one.wait()
        st[at + 1] = st[at] + st_in[at, 0] + st_in[at, 1] + st_in[at, 2]

    def main():
        yield from forward(1)
        mixture()
        yield
        out_project()
        copies = start([remote(st.at[0], st_in.at[0, k], peer) for k, peer in enumerate(t_peers)])
        yield
        turn_attention(1)
        targets()
        sum_up(copies, t_peers, 0)
        copies = start([remote(st.at[1], st_in.at[1, k], peer) for k, peer in enumerate(b_peers)])
        yield
        prepare(1)
        sum_up(copies, b_peers, 1)
        copies = start([remote(st.at[2], st_in.at[2, k], peer) for k, peer in enumerate(a_peers)])
        yield
        sum_up(copies, a_peers, 2)
        upstream(st[3])
        for layer in (1, 0):
            unmix(layer)
            turn = 2 + layer
            steps = scatter(layer, turn)
            next(steps)
            yield
            next(steps)
            out_grad(layer)
            yield
            yield from steps
            gr_all[layer, c, a, b] = scattered(turn).astype(BF16)
            steps = gather(gr_all.at[layer])
            next(steps)
            yield
            next(steps)
            if layer == 0:
                small_grads(1)
            yield
            yield from steps
            norm_back(layer)
            if layer == 1:
                input_grad(1)
        small_grads(0)
        yield

    def background():
        yield from forward(0)
        turn_attention(0)
        yield
        prepare(0)
        yield

    gains[pipe, 0:8, :] = jnp.broadcast_to(gain_ref[:, rows_of(dp * 128, 128)], (8, 128))
    loads[0].wait()
    cross = [
        remote(gains.at[pipe], gains.at[pipe], pipe_peer),
        remote(wvb.at[pipe], wvb.at[pipe], pipe_peer),
    ]
    send_x(1)
    start(cross)
    attend()
    att_cross.start()
    att_all[pipe, c, a, b, xh] = att_own[pipe]
    for m in range(4):
        rows = x_ref[m * 32:(m + 1) * 32, :].astype(F32)
        sq[m] = jnp.broadcast_to(jnp.sum(rows * rows, axis=1, keepdims=True), (32, 128))
    sq_in[pipe, tensor] = sq[pipe * 2 + c]
    squares = []
    for peer in t_peers:
        own = lax.rem(peer["tensor"], 2)
        squares.append(remote(sq.at[pipe * 2 + own], sq_in.at[pipe, tensor], peer))
        squares.append(remote(
            sq.at[other * 2 + own], sq_in.at[pipe, tensor], {"tensor": peer["tensor"], "pipe": other}
        ))
    squares.append(remote(sq.at[other * 2 + c], sq_in.at[pipe, tensor], pipe_peer))
    start(squares)
    attention1 = gather_attention(1)
    next(attention1)
    loads[1].wait()

    def turn_w(layer):
        def body(k, carry):
            wq[layer, rows_of(k * 128, 128), :] = wb[layer, rows_of(k * 128, 128), :].T
            return carry

        lax.fori_loop(0, 32, body, 0)
        for k in range(4):
            wvt[layer, k * 128:(k + 1) * 128, :] = wvb[layer, :, k * 128:(k + 1) * 128].T

    v_bd[...] = jnp.zeros_like(v_bd)
    up_bd[...] = jnp.zeros_like(up_bd)
    finish(squares)
    for layer in range(2):
        squared = sq_in[layer, 0] + sq_in[layer, 1] + sq_in[layer, 2] + sq_in[layer, 3]
        rms_own[layer] = lax.rsqrt(squared / D + EPS)
    finish(cross)
    next(attention1)

    @pl.when(pipe == 1)
    def _():
        att_cross.wait_send()

    w_copies = [
        remote(wb.at[pipe, k * 512:(k + 1) * 512], wb.at[pipe, k * 512:(k + 1) * 512], pipe_peer)
        for k in range(8)
    ]

    def pieces(copies, sender):
        for one in copies:
            @pl.when(pipe == sender)
            def _():
                one.start()

            yield

    def weights(layer):
        for _ in pieces(w_copies, layer):
            yield
        for one in w_copies:
            @pl.when(pipe == layer)
            def _():
                one.wait_send()

            @pl.when(pipe != layer)
            def _():
                one.wait_recv()

        yield
        turn_w(layer)
        yield

    def send_other_x():
        send_x(0)
        yield

    streams = {
        "m": main(), "g": background(), "a": attention1, "b": gather_attention(0),
        "w": weights(1), "u": weights(0), "s": send_other_x(),
        "o": pieces(go_copies, 0), "q": pieces(go_copies, 1),
    }
    for names in ORDER:
        for name in names:
            next(streams[name])

    @pl.when(pipe == 0)
    def _():
        att_cross.wait_send()

    for one in go_copies:
        one.wait()
    keep.wait()
    gv_copy.wait()
    gg_copy.wait()
    gv_ref[...] = (gv_own[...] + gv_in[...].astype(F32)).astype(BF16)
    gg_ref[...] = jnp.sum(gg_own[...] + gg_in[...], axis=0, keepdims=True)


def add_halves(own_ref, other_ref, value_ref, gain_ref, go_ref, gv_ref, gg_ref):
    go_ref[...] = (own_ref[...].astype(F32) + other_ref[...].astype(F32)).astype(BF16)

    @pl.when(pl.program_id(0) == 0)
    def _():
        gv_ref[...] = value_ref[...]
        gg_ref[...] = gain_ref[...]


def shards(
    layer_inputs, norm_gain, value_weight, out_weight, scores, head_weight, lengths, returns,
    response_mask,
):
    vmem = pl.BlockSpec(memory_space=pltpu.VMEM)
    anywhere = pl.BlockSpec(memory_space=pl.ANY)
    smem = pl.BlockSpec(memory_space=pltpu.SMEM)

    def scratch(*shape, dtype=BF16):
        return pltpu.VMEM(shape, dtype)

    own_out, other_out, grad_value, grad_gain = pl.pallas_call(
        kernel,
        out_shape=(
            jax.ShapeDtypeStruct((4096, 128), BF16),
            jax.ShapeDtypeStruct((4096, 128), BF16),
            jax.ShapeDtypeStruct((128, 512), BF16),
            jax.ShapeDtypeStruct((1, 128), F32),
        ),
        in_specs=[vmem, smem, vmem, vmem, vmem, vmem, anywhere, anywhere, vmem],
        out_specs=(anywhere, anywhere, vmem, vmem),
        scratch_shapes=[
            scratch(2, 144, 128),
            scratch(2, 2, 4, 4, 2, 144, 128),
            scratch(2, 2, 4, 4, 32, 640),
            scratch(2, 1024, 128),
            scratch(2, 2, 4, 4, 32, 512),
            scratch(4, 4, 32, 512),
            scratch(4, 4, 4, 32, 512),
            scratch(4, 3, 4, 32, 512),
            scratch(4, 3, 32, 512),
            scratch(4, 4, 32, 512),
            scratch(2, 2, 4, 4, 32, 512),
            scratch(4, 32, 128, dtype=F32),
            scratch(2, 4, 32, 128, dtype=F32),
            scratch(2, 1024, 4096),
            scratch(2, 16, 2, 256, 128),
            scratch(4, 4, 128, 512),
            scratch(2, 128, 512),
            scratch(2, 4096, 128),
            scratch(2, 4096, 128),
            scratch(2, 128, 512),
            scratch(2, 512, 128),
            scratch(2, 8, 128, dtype=F32),
            scratch(2, 32, 128, dtype=F32),
            scratch(2, 1024, 128, dtype=F32),
            scratch(1024, 128, dtype=F32),
            scratch(4, 16, 128, dtype=F32),
            scratch(3, 3, 16, 128, dtype=F32),
            scratch(128, 128, dtype=F32),
            scratch(32, 128, dtype=F32),
            scratch(2, 2, 8, 128, dtype=F32),
            scratch(2, 1024, 128),
            scratch(2, 1024, 128, dtype=F32),
            scratch(2, 1024, 512),
            scratch(2, 4, 128, 1024),
            scratch(2, 128, 1024),
            scratch(4096, 128),
            scratch(4096, 128),
            scratch(128, 512, dtype=F32),
            scratch(128, 512),
            scratch(128, 512),
            scratch(8, 128, dtype=F32),
            scratch(8, 128, dtype=F32),
            scratch(8, 128, dtype=F32),
            pltpu.SemaphoreType.DMA((COPIES,)),
            pltpu.SemaphoreType.DMA((COPIES,)),
            pltpu.SemaphoreType.DMA((3,)),
        ],
        compiler_params=pltpu.CompilerParams(
            collective_id=0, has_side_effects=True, vmem_limit_bytes=60 * 1024 * 1024
        ),
        cost_estimate=pl.CostEstimate(
            flops=8_000_000_000, bytes_accessed=6_000_000, transcendentals=0
        ),
    )(
        scores[0, 0],
        lengths.T,
        returns.reshape(1, 128),
        response_mask.reshape(1, 128),
        layer_inputs[0],
        norm_gain,
        value_weight[0],
        out_weight[0],
        head_weight.reshape(16, 128),
    )
    piece = pl.BlockSpec((2048, 128), lambda k: (k, 0))
    value_block = pl.BlockSpec((128, 512), lambda k: (0, 0))
    gain_block = pl.BlockSpec((1, 128), lambda k: (0, 0))
    grad_out, grad_value, grad_gain = pl.pallas_call(
        add_halves,
        out_shape=(
            jax.ShapeDtypeStruct((4096, 128), BF16),
            jax.ShapeDtypeStruct((128, 512), BF16),
            jax.ShapeDtypeStruct((1, 128), F32),
        ),
        grid=(2,),
        in_specs=[piece, piece, value_block, gain_block],
        out_specs=(piece, value_block, gain_block),
    )(own_out, other_out, grad_value, grad_gain)
    return grad_out[None], grad_value[None], grad_gain


def solution(mesh):
    return jax.shard_map(
        shards,
        mesh=mesh,
        in_specs=(
            P("pipe", "dp", "tensor"),
            P("pipe", "tensor"),
            P("pipe", ("tensor", "dp"), None),
            P("pipe", None, ("tensor", "dp")),
            P("pipe", "dp", None, "tensor", None, None),
            P("tensor"),
            P(),
            P("dp"),
            P("dp"),
        ),
        out_specs=(
            P("pipe", None, ("tensor", "dp")),
            P("pipe", ("tensor", "dp"), None),
            P("pipe", ("tensor", "dp")),
        ),
        check_vma=False,
    )
```
